128 devices in a mesh: dp: 8 (over y_lo, x), ctx: 16 (over z, y_hi, core).
Axes of the slice: x: 4, y: 4 (y_hi: 2, y_lo: 2; y = y_hi * 2 + y_lo), z: 4, core: 2. Of those that a mesh axis runs over, the one named last changes fastest.
Arguments:
- hidden: bfloat16 [32768, 8192], P(('dp', 'ctx')), may hold values from -0.5 to 0.5
- queries: bfloat16 [32768, 512], P(('dp', 'ctx')), may hold values from -13 to 13
- key_rows: bfloat16 [32768, 128], P(('dp', 'ctx')), may hold values from -6 to 6
- value_rows: bfloat16 [32768, 128], P(('dp', 'ctx')), may hold values from -6 to 6
- out_grad: bfloat16 [32768, 512], P(('dp', 'ctx')), may hold values from -6 to 6
- doc_ids: int32 [32768], P(('dp', 'ctx')), may hold values from 4095 to 32767, as said below
- q_weight: bfloat16 [8192, 512], replicated, may hold values from -0.25 to 0.25
- k_weight: bfloat16 [8192, 128], replicated, may hold values from -0.5 to 0.5
- v_weight: bfloat16 [8192, 128], replicated, may hold values from -0.5 to 0.5
Outputs:
- input_grad: bfloat16 [32768, 8192], P(('dp', 'ctx'))
- kv_weight_grad: float32 [8192, 256], P(('dp', 'ctx'))
The draws below stay inside these ranges and needn't reach their ends.
Inputs may be any that keep to these rules, and one draw needn't show every extreme that they name: `doc_ids`: A token's number is 4096 times its row along dp plus the index within that row of its document's last token; a document never leaves its row along dp.
All inputs are finite; a program needn't handle non-finite values.
Results may differ from the reference program's by a relative error of at most 0.0058.
Values may be sent and summed in bfloat16 or wider, within the bound.
A program may use at most 128 MiB of HBM per device.

```python
import jax
import jax.numpy as jnp
from jax import lax

D = 8192
HD = 128
HQ = 4
TOK_DEV = 256
SEQ = 4096
TOKENS = 32768
N_DP = 8
N_CTX = 16


def draw_queries(key, part):
    key = jax.random.fold_in(key, 3)
    drawn = jnp.clip(jax.random.normal(key, (TOKENS, HQ * HD), jnp.float32), -6.0, 6.0)
    return drawn.astype(jnp.bfloat16)


def draw_key_rows(key, part):
    key = jax.random.fold_in(key, 5)
    drawn = jnp.clip(jax.random.normal(key, (TOKENS, HD), jnp.float32), -6.0, 6.0)
    return drawn.astype(jnp.bfloat16)


def draw_doc_ids(key, part):
    key = jax.random.fold_in(key, 11)
    cut_key, break_key = jax.random.split(key)
    cuts = jax.random.randint(cut_key, (N_DP, N_CTX), 0, 2)
    device = jnp.arange(N_CTX)[None, :]
    row_number = jnp.arange(N_DP)[:, None]
    cuts = jnp.where(device == 0, 1, jnp.where(row_number == 0, 0, cuts))
    after = jnp.concatenate([cuts[:, 1:], jnp.ones((N_DP, 1), cuts.dtype)], axis=1)
    single = (cuts == 1) & (after == 1)
    place = jnp.arange(TOK_DEV)
    breaks = jax.random.randint(break_key, (N_DP, N_CTX, TOK_DEV), 0, 2)
    begins = (place == 0)[None, None, :] & (cuts == 1)[:, :, None] | single[:, :, None] & (place % 16 == 0)[None, None, :] & (breaks == 1)
    begins = begins.reshape(N_DP, SEQ)
    follows = jnp.concatenate([begins[:, 1:], jnp.ones((N_DP, 1), bool)], axis=1)
    position = jnp.arange(SEQ, dtype=jnp.int32)
    endings = jnp.where(follows, position[None, :], SEQ)
    last_token = lax.cummin(endings, axis=1, reverse=True)
    return (last_token + row_number * SEQ).reshape(TOKENS).astype(jnp.int32)


def strengthened(array, key, source, target, shards_of, factor):
    def block_of(dim):
        return (jnp.arange(array.shape[dim]) // (array.shape[dim] // shards_of)).reshape((-1,) + (1,) * (array.ndim - 1 - dim))

    near = jax.random.permutation(key, shards_of)[block_of(target)]
    far = (block_of(target) + shards_of // 2) % shards_of
    return jnp.where((block_of(source) == near) | (block_of(source) == far), factor * array, array)


def levels(stream_key, shape, shards, low, top_value):
    factor_of = 1.0
    for dim, parts in shards:
        heights = jax.random.uniform(jax.random.fold_in(jax.random.fold_in(stream_key, 6), dim), (parts,), jnp.float32, low / len(shards), top_value / len(shards))
        factor_of = factor_of * jnp.repeat(jnp.exp(heights), shape[dim] // parts).reshape((-1,) + (1,) * (len(shape) - 1 - dim))
    return factor_of


def scatter_about(key, extent, spread, reach, cuts=(), held_as=jnp.bfloat16):
    values = jax.random.normal(key, extent, jnp.float32) * spread
    if len(cuts) > 0:
        values = levels(key, extent, cuts, -0.22, 0.18) * values
    return jnp.clip(values, min=-reach, max=reach).astype(held_as)


def heavy_noise(rng, extent, deviation, reach, shards, heavy, held_as=jnp.bfloat16):
    result = deviation * jax.random.normal(rng, extent, jnp.float32)
    if shards:
        result = result * levels(rng, extent, shards, -0.22, 0.18)
    return jnp.clip(strengthened(result, jax.random.fold_in(rng, 3), *heavy), -reach, reach).astype(held_as)


def setup_inputs(seed: int = 0) -> dict:
    streams_of = jax.random.split(jax.random.key(seed), 10)
    return {
        "hidden": heavy_noise(streams_of[0], (TOKENS, D), 0.02, 0.5, ((0, 128),), (0, 1, 128, 5.5)),
        "queries": draw_queries(jax.random.fold_in(streams_of[9], 71), 0),
        "key_rows": draw_key_rows(jax.random.fold_in(streams_of[9], 71), 0),
        "value_rows": scatter_about(streams_of[3], (TOKENS, HD), 1.0, 6.0, ((0, 128),)),
        "out_grad": scatter_about(streams_of[4], (TOKENS, HQ * HD), 1.0, 6.0, ((0, 128),)),
        "doc_ids": draw_doc_ids(jax.random.fold_in(streams_of[9], 71), 0),
        "q_weight": scatter_about(streams_of[6], (D, HQ * HD), (HQ * HD) ** -0.5, 0.25),
        "k_weight": scatter_about(streams_of[7], (D, HD), HD ** -0.5, 0.5),
        "v_weight": scatter_about(streams_of[8], (D, HD), HD ** -0.5, 0.5),
    }


def head_grads(query_head, grad_head, row_keys, row_values, allowed, score_scale):
    scores = jnp.dot(query_head, row_keys.T, preferred_element_type=jnp.float32) * score_scale
    scores = jnp.where(allowed, scores, -jnp.inf)
    row_max = jnp.max(scores, axis=1, keepdims=True)
    probs = jnp.exp(scores - row_max)
    probs = probs / jnp.sum(probs, axis=1, keepdims=True)
    probs_low = probs.astype(jnp.bfloat16)
    output = jnp.dot(probs_low, row_values, preferred_element_type=jnp.float32)
    row_delta = jnp.sum(grad_head.astype(jnp.float32) * output, axis=1, keepdims=True)
    value_grad = jnp.dot(probs_low.T, grad_head, preferred_element_type=jnp.float32)
    prob_grad = jnp.dot(grad_head, row_values.T, preferred_element_type=jnp.float32)
    score_grad = (score_scale * probs * (prob_grad - row_delta)).astype(jnp.bfloat16)
    query_grad = jnp.dot(score_grad, row_keys, preferred_element_type=jnp.float32)
    key_grad = jnp.dot(score_grad.T, query_head, preferred_element_type=jnp.float32)
    return query_grad, key_grad, value_grad


def reference(hidden, queries, key_rows, value_rows, out_grad, doc_ids, q_weight, k_weight, v_weight):
    score_scale = HD ** -0.5
    position = jnp.arange(SEQ, dtype=jnp.int32)

    def row_grads(pieces):
        row_queries, row_keys, row_values, row_out_grad, row_docs = pieces
        allowed = (row_docs[:, None] == row_docs[None, :]) & (position[None, :] <= position[:, None])
        query_heads = row_queries.reshape(SEQ, HQ, HD).transpose(1, 0, 2)
        grad_heads = row_out_grad.reshape(SEQ, HQ, HD).transpose(1, 0, 2)

        def per_head(head_pieces):
            return head_grads(head_pieces[0], head_pieces[1], row_keys, row_values, allowed, score_scale)

        query_grad, key_grad, value_grad = lax.map(per_head, (query_heads, grad_heads))
        query_grad = query_grad.transpose(1, 0, 2).reshape(SEQ, HQ * HD)
        return query_grad, jnp.sum(key_grad, axis=0), jnp.sum(value_grad, axis=0)

    query_grad, key_grad, value_grad = lax.map(row_grads, (
        queries.reshape(N_DP, SEQ, HQ * HD),
        key_rows.reshape(N_DP, SEQ, HD),
        value_rows.reshape(N_DP, SEQ, HD),
        out_grad.reshape(N_DP, SEQ, HQ * HD),
        doc_ids.reshape(N_DP, SEQ)))
    query_grad = query_grad.reshape(TOKENS, HQ * HD).astype(jnp.bfloat16)
    key_grad = key_grad.reshape(TOKENS, HD).astype(jnp.bfloat16)
    value_grad = value_grad.reshape(TOKENS, HD).astype(jnp.bfloat16)
    input_grad = jnp.dot(query_grad, q_weight.T, preferred_element_type=jnp.float32)
    input_grad = input_grad + jnp.dot(key_grad, k_weight.T, preferred_element_type=jnp.float32)
    input_grad = input_grad + jnp.dot(value_grad, v_weight.T, preferred_element_type=jnp.float32)
    kv_grads = jnp.concatenate([key_grad, value_grad], axis=1)
    kv_weight_grad = jnp.dot(hidden.T, kv_grads, preferred_element_type=jnp.float32)
    return input_grad.astype(jnp.bfloat16), kv_weight_grad
```

```python
import functools

import jax
import jax.numpy as jnp
from jax import lax
from jax.experimental import pallas as pl
from jax.experimental.pallas import tpu as pltpu
from jax.sharding import PartitionSpec as P

MESH = pl.DeviceIdType.MESH
BF16 = jnp.bfloat16
F32 = jnp.float32
LOG2E = 1.4426950408889634
MASKED = -1e30


def dot(a, b):
    return jnp.dot(a, b, preferred_element_type=F32)


def attention_kernel(
    seq, q_ref, k_ref, v_ref, do_ref, docs_ref, dq_ref, dkv_ref,
    kv, q_t, do_t, probs, max_at, run_max, run_sum, out_t, delta, dq_t, acc,
    pair_out, pair_in, far_out, far_in,
    kv_send, kv_relay, kv_recv, pair_send, pair_recv, far_send, far_recv,
):
    tok, head = k_ref.shape
    heads = q_ref.shape[1] // head
    chips = kv.shape[0] // 2
    scale = head ** -0.5
    row = lax.axis_index("dp")
    me = lax.axis_index("ctx")
    chip, core = me // 2, me % 2
    other = 1 - core
    partner = chip * 2 + other

    def at(ctx):
        return (row, ctx)

    kv[me, 0:tok, 0:head] = k_ref[...]
    kv[me, 0:tok, head : 2 * head] = v_ref[...]
    last = docs_ref[...] - row * seq
    high, low = last // 64, last % 64
    digit = lax.broadcasted_iota(jnp.int32, (16, tok), 0)
    kv[me, tok : tok + 16, :] = jnp.where(digit == 0, high, low).astype(F32).astype(BF16)
    own_docs = last.astype(F32)

    barrier = pltpu.get_barrier_semaphore()
    for step in range(1, chips):
        peer = lax.rem(chip + step, chips) * 2 + core
        pl.semaphore_signal(barrier, inc=1, device_id=at(peer), device_id_type=MESH)
    pl.semaphore_signal(barrier, inc=1, device_id=at(partner), device_id_type=MESH)
    pl.semaphore_wait(barrier, chips)

    def kv_copy(slot, send_sem, target):
        return pltpu.make_async_remote_copy(
            src_ref=kv.at[slot], dst_ref=kv.at[slot], send_sem=send_sem,
            recv_sem=kv_recv.at[slot], device_id=at(target), device_id_type=MESH)

    def pair_copy(index):
        return pltpu.make_async_remote_copy(
            src_ref=pair_out.at[index], dst_ref=pair_in.at[index], send_sem=pair_send.at[index],
            recv_sem=pair_recv.at[index], device_id=at(partner), device_id_type=MESH)

    def far_copy(index, slot):
        return pltpu.make_async_remote_copy(
            src_ref=far_out.at[index], dst_ref=far_in.at[slot], send_sem=far_send.at[index],
            recv_sem=far_recv.at[slot], device_id=at(index * 2 + core), device_id_type=MESH)

    @pl.when(core == 0)
    def _():
        kv_copy(me, kv_send.at[chip], partner).start()

    @pl.loop(chip + 1, chips)
    def _(target):
        kv_copy(me, kv_send.at[target], target * 2 + core).start()

    for h in range(heads):
        cols = slice(h * head, (h + 1) * head)
        rows = slice(h * tok, (h + 1) * tok)
        q_t[:, rows] = q_ref[:, cols].T
        do_t[:, rows] = do_ref[:, cols].T
    run_max[...] = jnp.full_like(run_max, MASKED)
    run_sum[...] = jnp.zeros_like(run_sum)
    out_t[...] = jnp.zeros_like(out_t)
    dq_t[...] = jnp.zeros_like(dq_t)

    @pl.loop(0, 2 * (chip + 1))
    def _(i):
        back, second = i // 2, i % 2
        source = chip - back
        slot = 2 * source + jnp.where(second == 0, core, other)
        skipped = (i == 1) & (core == 0)

        @pl.when((i > 0) & jnp.logical_not(skipped))
        def _():
            kv_copy(slot, kv_relay.at[source], partner).wait_recv()

        @pl.when((i > 0) & (second == 0))
        def _():
            kv_copy(slot, kv_relay.at[source], partner).start()

        @pl.when(jnp.logical_not(skipped))
        def _():
            keys = kv[slot, 0:tok, 0:head]
            values_t = kv[slot, 0:tok, head : 2 * head].T
            digits = kv[slot, tok : tok + 16, :].astype(F32)
            key_docs = digits[0:1, :] * 64.0 + digits[1:2, :]
            key_docs = jnp.broadcast_to(key_docs, (tok, tok)).T
            key_pos = lax.broadcasted_iota(jnp.int32, (tok, tok), 0)
            query_pos = lax.broadcasted_iota(jnp.int32, (tok, tok), 1)
            allowed = (key_docs == own_docs) & (key_pos - query_pos <= (me - slot) * tok)
            for h in range(heads):
                rows = slice(h * tok, (h + 1) * tok)
                scores = dot(keys, q_t[:, rows]) * (scale * LOG2E)
                scores = jnp.where(allowed, scores, MASKED)
                old_max = run_max[:, rows]
                new_max = jnp.maximum(old_max, jnp.max(scores, axis=0, keepdims=True))
                weights = jnp.exp2(scores - new_max)
                shrink = jnp.exp2(old_max - new_max)
                run_max[:, rows] = new_max
                max_at[slot, :, rows] = new_max
                run_sum[:, rows] = run_sum[:, rows] * shrink + jnp.sum(weights, axis=0, keepdims=True)
                probs[slot, :, rows] = weights
                out_t[:, rows] = out_t[:, rows] * shrink + dot(values_t, weights.astype(BF16))

    run_sum[...] = 1.0 / run_sum[...]
    delta[...] = run_sum[...] * jnp.sum(out_t[...] * do_t[...].astype(F32), axis=0, keepdims=True)

    @pl.loop(0, 2 * (chip + 1))
    def _(i):
        source, second = i // 2, i % 2
        slot = 2 * source + jnp.where(second == 0, other, core)
        own_chip = source == chip
        skipped = own_chip & (second == 0) & (core == 0)

        @pl.when(jnp.logical_not(skipped))
        def _():
            keys_t = kv[slot, 0:tok, 0:head].T
            values = kv[slot, 0:tok, head : 2 * head]
            key_part = jnp.zeros((tok, head), F32)
            value_part = jnp.zeros((tok, head), F32)
            for h in range(heads):
                cols = slice(h * head, (h + 1) * head)
                rows = slice(h * tok, (h + 1) * tok)
                factor = jnp.exp2(max_at[slot, :, rows] - run_max[:, rows]) * run_sum[:, rows]
                prob = probs[slot, :, rows] * factor
                prob_grad = dot(values, do_t[:, rows])
                score_grad = (scale * prob * (prob_grad - delta[:, rows])).astype(BF16)
                value_part += dot(prob.astype(BF16), do_ref[:, cols])
                key_part += dot(score_grad, q_ref[:, cols])
                dq_t[:, rows] += dot(keys_t, score_grad)
            acc[:, 0:head] = key_part
            acc[:, head : 2 * head] = value_part

        @pl.when((second == 0) & jnp.logical_not(skipped))
        def _():
            pair_out[source] = acc[...].astype(BF16)
            pair_copy(source).start()

        @pl.when((second == 1) & jnp.logical_not(own_chip))
        def _():
            pair_copy(source).wait_recv()
            far_out[source] = (acc[...] + pair_in[source].astype(F32)).astype(BF16)
            far_copy(source, chip).start()

    for h in range(heads):
        cols = slice(h * head, (h + 1) * head)
        rows = slice(h * tok, (h + 1) * tok)
        dq_ref[:, cols] = dq_t[:, rows].T.astype(BF16)

    @pl.when(core == 0)
    def _():
        pair_copy(chip).wait_recv()
        acc[...] += pair_in[chip].astype(F32)

    @pl.loop(chip + 1, chips)
    def _(source):
        far_copy(source, source).wait_recv()
        acc[...] += far_in[source].astype(F32)

    dkv_ref[...] = acc[...].astype(BF16)

    @pl.when(core == 0)
    def _():
        kv_copy(me, kv_send.at[chip], partner).wait_send()

    @pl.when(core == 1)
    def _():
        pair_copy(chip).wait_send()

    @pl.loop(chip + 1, chips)
    def _(target):
        kv_copy(me, kv_send.at[target], target * 2 + core).wait_send()

    @pl.loop(0, chip)
    def _(source):
        kv_copy(2 * source + core, kv_relay.at[source], partner).wait_send()
        pair_copy(source).wait_send()
        far_copy(source, chip).wait_send()


def attention_grads(queries, key_rows, value_rows, out_grad, docs, n_ctx):
    tok, head = key_rows.shape
    width = queries.shape[1]
    heads = width // head
    chips = n_ctx // 2
    vmem = pl.BlockSpec(memory_space=pltpu.VMEM)
    dma = pltpu.SemaphoreType.DMA
    return pl.pallas_call(
        functools.partial(attention_kernel, tok * n_ctx),
        out_shape=(
            jax.ShapeDtypeStruct((tok, width), BF16),
            jax.ShapeDtypeStruct((tok, 2 * head), BF16),
        ),
        in_specs=[vmem] * 5,
        out_specs=(vmem, vmem),
        scratch_shapes=[
            pltpu.VMEM((n_ctx, tok + 16, 2 * head), BF16),
            pltpu.VMEM((head, heads * tok), BF16),
            pltpu.VMEM((head, heads * tok), BF16),
            pltpu.VMEM((n_ctx, tok, heads * tok), F32),
            pltpu.VMEM((n_ctx, 1, heads * tok), F32),
            pltpu.VMEM((1, heads * tok), F32),
            pltpu.VMEM((1, heads * tok), F32),
            pltpu.VMEM((head, heads * tok), F32),
            pltpu.VMEM((1, heads * tok), F32),
            pltpu.VMEM((head, heads * tok), F32),
            pltpu.VMEM((tok, 2 * head), F32),
            pltpu.VMEM((chips, tok, 2 * head), BF16),
            pltpu.VMEM((chips, tok, 2 * head), BF16),
            pltpu.VMEM((chips, tok, 2 * head), BF16),
            pltpu.VMEM((chips, tok, 2 * head), BF16),
            dma((chips,)), dma((chips,)), dma((n_ctx,)),
            dma((chips,)), dma((chips,)), dma((chips,)), dma((chips,)),
        ],
        compiler_params=pltpu.CompilerParams(
            collective_id=0, has_side_effects=True, vmem_limit_bytes=56 * 1024 * 1024
        ),
    )(queries, key_rows, value_rows, out_grad, docs)


def project_back(grad_rows, weight):
    return lax.dot_general(
        grad_rows, weight, (((1,), (1,)), ((), ())), preferred_element_type=F32
    )


def on_device(
    n_ctx, hidden, queries, key_rows, value_rows, out_grad, doc_ids, q_weight, k_weight, v_weight
):
    head = key_rows.shape[1]
    query_grad, kv_grads = attention_grads(
        queries, key_rows, value_rows, out_grad, doc_ids.reshape(1, -1), n_ctx)
    key_grad, value_grad = kv_grads[:, :head], kv_grads[:, head:]
    input_grad = project_back(query_grad, q_weight) + project_back(key_grad, k_weight)
    input_grad = (input_grad + project_back(value_grad, v_weight)).astype(BF16)
    kv_weight_grad = lax.psum_scatter(
        lax.dot_general(hidden, kv_grads, (((0,), (0,)), ((), ())), preferred_element_type=F32),
        ("dp", "ctx"),
        scatter_dimension=0,
        tiled=True,
    )
    return (input_grad, kv_weight_grad)


def solution(mesh):
    tokens = P(("dp", "ctx"), None)
    return jax.shard_map(
        functools.partial(on_device, mesh.shape["ctx"]),
        mesh=mesh,
        in_specs=(tokens, tokens, tokens, tokens, tokens, P(("dp", "ctx")), P(), P(), P()),
        out_specs=(tokens, tokens),
        check_vma=False,
    )
```

```python
import functools

import jax
import jax.numpy as jnp
from jax import lax
from jax.experimental import pallas as pl
from jax.experimental.pallas import tpu as pltpu
from jax.sharding import PartitionSpec as P

MESH = pl.DeviceIdType.MESH
BF16 = jnp.bfloat16
F32 = jnp.float32
LOG2E = 1.4426950408889634
MASKED = -1e30


def dot(a, b):
    return jnp.dot(a, b, preferred_element_type=F32)


def dot_rows(a, b):
    return lax.dot_general(a, b, (((1,), (1,)), ((), ())), preferred_element_type=F32)


def backward_kernel(
    seq, q_ref, k_ref, v_ref, do_ref, docs_ref, hidden_ref, qw_ref, kw_ref, vw_ref,
    grad_ref, wgrad_ref,
    kv, q_t, do_t, probs, max_at, run_max, run_sum, out_t, delta, dq_t, acc,
    pair_out, pair_in, far_out, far_in,
    wide, hidden_t, hidden_in, qw, kw, vw, dq, dkv,
    sum1_x, sum1_y, sum1_z, got1_x, got1_y, got1_z,
    sum2_x, sum2_y, sum2_z, got2_x, got2_y, got2_z,
    sum3_x, sum3_y, sum3_z, got3_x, got3_y, got3_z,
    kv_send, kv_relay, kv_recv, pair_send, pair_recv, far_send, far_recv,
    load_sem, store_sem, core_send, core_recv, ring_send, ring_recv,
):
    tok, head = k_ref.shape
    heads = q_ref.shape[1] // head
    chips = kv.shape[0] // 2
    scale = head ** -0.5
    row = lax.axis_index("dp")
    me = lax.axis_index("ctx")
    chip, core = me // 2, me % 2
    other = 1 - core
    partner = chip * 2 + other
    place = (row % 4, (chip % 2) * 2 + row // 4, chip // 2)

    def at(ctx):
        return (row, ctx)

    def along(axis, step):
        x, y, z = [lax.rem(p + step, 4) if i == axis else p for i, p in enumerate(place)]
        return ((y % 2) * 4 + x, z * 4 + (y // 2) * 2 + core)

    loads = [
        pltpu.make_async_copy(src, dst, load_sem.at[i])
        for i, (src, dst) in enumerate(
            ((hidden_ref, wide), (qw_ref, qw), (kw_ref, kw), (vw_ref, vw)))
    ]
    for load in loads:
        load.start()

    kv[me, 0:tok, 0:head] = k_ref[...]
    kv[me, 0:tok, head : 2 * head] = v_ref[...]
    last = docs_ref[...] - row * seq
    high, low = last // 64, last % 64
    digit = lax.broadcasted_iota(jnp.int32, (16, tok), 0)
    kv[me, tok : tok + 16, :] = jnp.where(digit == 0, high, low).astype(F32).astype(BF16)
    own_docs = last.astype(F32)

    barrier = pltpu.get_barrier_semaphore()
    for step in range(1, chips):
        peer = lax.rem(chip + step, chips) * 2 + core
        pl.semaphore_signal(barrier, inc=1, device_id=at(peer), device_id_type=MESH)
    pl.semaphore_signal(barrier, inc=1, device_id=at(partner), device_id_type=MESH)
    for axis, step in ((0, 1), (0, 2), (0, 3), (1, 1), (1, 3)):
        pl.semaphore_signal(barrier, inc=1, device_id=along(axis, step), device_id_type=MESH)
    pl.semaphore_wait(barrier, chips + 5)

    def kv_copy(slot, send_sem, target):
        return pltpu.make_async_remote_copy(
            src_ref=kv.at[slot], dst_ref=kv.at[slot], send_sem=send_sem,
            recv_sem=kv_recv.at[slot], device_id=at(target), device_id_type=MESH)

    def pair_copy(index):
        return pltpu.make_async_remote_copy(
            src_ref=pair_out.at[index], dst_ref=pair_in.at[index], send_sem=pair_send.at[index],
            recv_sem=pair_recv.at[index], device_id=at(partner), device_id_type=MESH)

    def far_copy(index, slot):
        return pltpu.make_async_remote_copy(
            src_ref=far_out.at[index], dst_ref=far_in.at[slot], send_sem=far_send.at[index],
            recv_sem=far_recv.at[slot], device_id=at(index * 2 + core), device_id_type=MESH)

    @pl.when(core == 0)
    def _():
        kv_copy(me, kv_send.at[chip], partner).start()

    @pl.loop(chip + 1, chips)
    def _(target):
        kv_copy(me, kv_send.at[target], target * 2 + core).start()

    for h in range(heads):
        cols = slice(h * head, (h + 1) * head)
        rows = slice(h * tok, (h + 1) * tok)
        q_t[:, rows] = q_ref[:, cols].T
        do_t[:, rows] = do_ref[:, cols].T
    run_max[...] = jnp.full_like(run_max, MASKED)
    run_sum[...] = jnp.zeros_like(run_sum)
    out_t[...] = jnp.zeros_like(out_t)
    dq_t[...] = jnp.zeros_like(dq_t)

    loads[0].wait()

    @pl.loop(0, hidden_t.shape[0])
    def _(group):
        turned = wide[:, pl.ds(pl.multiple_of(group * 128, 128), 128)].T
        hidden_t[group, 0] = turned[0:64]
        hidden_t[group, 1] = turned[64:128]

    hidden_copy = pltpu.make_async_remote_copy(
        src_ref=hidden_t.at[:, other], dst_ref=hidden_in, send_sem=core_send.at[0],
        recv_sem=core_recv.at[0], device_id=at(partner), device_id_type=MESH)
    hidden_copy.start()

    @pl.loop(0, 2 * (chip + 1))
    def _(i):
        back, second = i // 2, i % 2
        source = chip - back
        slot = 2 * source + jnp.where(second == 0, core, other)
        skipped = (i == 1) & (core == 0)

        @pl.when((i > 0) & jnp.logical_not(skipped))
        def _():
            kv_copy(slot, kv_relay.at[source], partner).wait_recv()

        @pl.when((i > 0) & (second == 0))
        def _():
            kv_copy(slot, kv_relay.at[source], partner).start()

        @pl.when(jnp.logical_not(skipped))
        def _():
            keys = kv[slot, 0:tok, 0:head]
            values_t = kv[slot, 0:tok, head : 2 * head].T
            digits = kv[slot, tok : tok + 16, :].astype(F32)
            key_docs = digits[0:1, :] * 64.0 + digits[1:2, :]
            key_docs = jnp.broadcast_to(key_docs, (tok, tok)).T
            key_pos = lax.broadcasted_iota(jnp.int32, (tok, tok), 0)
            query_pos = lax.broadcasted_iota(jnp.int32, (tok, tok), 1)
            allowed = (key_docs == own_docs) & (key_pos - query_pos <= (me - slot) * tok)
            for h in range(heads):
                rows = slice(h * tok, (h + 1) * tok)
                scores = dot(keys, q_t[:, rows]) * (scale * LOG2E)
                scores = jnp.where(allowed, scores, MASKED)
                old_max = run_max[:, rows]
                new_max = jnp.maximum(old_max, jnp.max(scores, axis=0, keepdims=True))
                weights = jnp.exp2(scores - new_max)
                shrink = jnp.exp2(old_max - new_max)
                run_max[:, rows] = new_max
                max_at[slot, :, rows] = new_max
                run_sum[:, rows] = run_sum[:, rows] * shrink + jnp.sum(weights, axis=0, keepdims=True)
                probs[slot, :, rows] = weights
                out_t[:, rows] = out_t[:, rows] * shrink + dot(values_t, weights.astype(BF16))

    run_sum[...] = 1.0 / run_sum[...]
    delta[...] = run_sum[...] * jnp.sum(out_t[...] * do_t[...].astype(F32), axis=0, keepdims=True)

    @pl.loop(0, 2 * (chip + 1))
    def _(i):
        source, second = i // 2, i % 2
        slot = 2 * source + jnp.where(second == 0, other, core)
        own_chip = source == chip
        skipped = own_chip & (second == 0) & (core == 0)

        @pl.when(jnp.logical_not(skipped))
        def _():
            keys_t = kv[slot, 0:tok, 0:head].T
            values = kv[slot, 0:tok, head : 2 * head]
            key_part = jnp.zeros((tok, head), F32)
            value_part = jnp.zeros((tok, head), F32)
            for h in range(heads):
                cols = slice(h * head, (h + 1) * head)
                rows = slice(h * tok, (h + 1) * tok)
                factor = jnp.exp2(max_at[slot, :, rows] - run_max[:, rows]) * run_sum[:, rows]
                prob = probs[slot, :, rows] * factor
                prob_grad = dot(values, do_t[:, rows])
                score_grad = (scale * prob * (prob_grad - delta[:, rows])).astype(BF16)
                value_part += dot(prob.astype(BF16), do_ref[:, cols])
                key_part += dot(score_grad, q_ref[:, cols])
                dq_t[:, rows] += dot(keys_t, score_grad)
            acc[:, 0:head] = key_part
            acc[:, head : 2 * head] = value_part

        @pl.when((second == 0) & jnp.logical_not(skipped))
        def _():
            pair_out[source] = acc[...].astype(BF16)
            pair_copy(source).start()

        @pl.when((second == 1) & jnp.logical_not(own_chip))
        def _():
            pair_copy(source).wait_recv()
            far_out[source] = (acc[...] + pair_in[source].astype(F32)).astype(BF16)
            far_copy(source, chip).start()

    for h in range(heads):
        cols = slice(h * head, (h + 1) * head)
        rows = slice(h * tok, (h + 1) * tok)
        dq[:, cols] = dq_t[:, rows].T.astype(BF16)

    @pl.when(core == 0)
    def _():
        pair_copy(chip).wait_recv()
        acc[...] += pair_in[chip].astype(F32)

    @pl.loop(chip + 1, chips)
    def _(source):
        far_copy(source, source).wait_recv()
        acc[...] += far_in[source].astype(F32)

    dkv[0] = acc[...].astype(BF16)
    dkv_copy = pltpu.make_async_remote_copy(
        src_ref=dkv.at[0], dst_ref=dkv.at[1], send_sem=core_send.at[1],
        recv_sem=core_recv.at[1], device_id=at(partner), device_id_type=MESH)
    dkv_copy.start()

    orders = ((0, 1, 2), (1, 2, 0), (2, 0, 1))
    sums = ((sum1_x, sum1_y, sum1_z), (sum2_x, sum2_y, sum2_z), (sum3_x, sum3_y, sum3_z))
    gots = ((got1_x, got1_y, got1_z), (got2_x, got2_y, got2_z), (got3_x, got3_y, got3_z))

    def ring_copy(stage, part, step):
        axis = orders[part][stage]
        return pltpu.make_async_remote_copy(
            src_ref=sums[stage][part].at[lax.rem(place[axis] + step, 4)],
            dst_ref=gots[stage][part].at[step - 1],
            send_sem=ring_send.at[stage, part, step - 1],
            recv_sem=ring_recv.at[stage, part, step - 1],
            device_id=along(axis, step), device_id_type=MESH)

    hidden_copy.wait_recv()
    dkv_copy.wait_recv()
    for step in (2, 1, 3, 0):
        x = lax.rem(place[0] + step, 4)
        for y_lo in range(2):
            groups = pl.ds(y_lo * 32 + x * 8, 8)
            own = hidden_t[groups, core].reshape(512, tok)
            paired = hidden_in[groups].reshape(512, tok)
            terms = (dot(own, dkv[0]) + dot(paired, dkv[1])).astype(BF16).reshape(4, 2, 64, 2 * head)
            for y_hi in range(2):
                y = y_hi * 2 + y_lo
                sum1_x[x, y] = terms[:, y_hi, 0:48, 0:head]
                sum1_y[y, :, x] = terms[:, y_hi, 0:48, head : 2 * head]
                sum1_z[:, x, y] = terms[:, y_hi, 48:64, :]
        if step > 0:
            ring_copy(0, 0, step).start()
    for part in (1, 2):
        for step in (2, 1, 3):
            ring_copy(0, part, step).start()

    for load in loads[1:]:
        load.wait()
    tile = 512

    def store_copy(index):
        cols = pl.ds(pl.multiple_of(index * tile, tile), tile)
        return pltpu.make_async_copy(wide.at[:, cols], grad_ref.at[:, cols], store_sem.at[index])

    @pl.loop(0, store_sem.shape[0])
    def _(index):
        rows = pl.ds(pl.multiple_of(index * tile, tile), tile)
        total = dot_rows(dq[...], qw[rows, :])
        total += dot_rows(dkv[0, :, 0:head], kw[rows, :])
        total += dot_rows(dkv[0, :, head : 2 * head], vw[rows, :])
        wide[:, rows] = total.astype(BF16)
        store_copy(index).start()

    for stage in range(3):
        for part in range(3):
            for step in (1, 3, 2):
                ring_copy(stage, part, step).wait_recv()
            mine = place[orders[part][stage]]
            total = sums[stage][part][mine].astype(F32)
            for step in range(3):
                total += gots[stage][part][step].astype(F32)
            if stage < 2:
                sums[stage + 1][part][...] = total.astype(sums[stage + 1][part].dtype)
                for step in (2, 1, 3):
                    ring_copy(stage + 1, part, step).start()
            else:
                wgrad_ref[(slice(0, 48), slice(0, 48), slice(48, 64))[part],
                          (slice(0, head), slice(head, 2 * head), slice(0, 2 * head))[part]] = total

    hidden_copy.wait_send()
    dkv_copy.wait_send()
    for stage in range(3):
        for part in range(3):
            for step in (1, 2, 3):
                ring_copy(stage, part, step).wait_send()

    @pl.loop(0, store_sem.shape[0])
    def _(index):
        store_copy(index).wait()

    @pl.when(core == 0)
    def _():
        kv_copy(me, kv_send.at[chip], partner).wait_send()

    @pl.when(core == 1)
    def _():
        pair_copy(chip).wait_send()

    @pl.loop(chip + 1, chips)
    def _(target):
        kv_copy(me, kv_send.at[target], target * 2 + core).wait_send()

    @pl.loop(0, chip)
    def _(source):
        kv_copy(2 * source + core, kv_relay.at[source], partner).wait_send()
        pair_copy(source).wait_send()
        far_copy(source, chip).wait_send()


def on_device(
    n_ctx, hidden, queries, key_rows, value_rows, out_grad, doc_ids, q_weight, k_weight, v_weight
):
    tok, head = key_rows.shape
    width = queries.shape[1]
    model = hidden.shape[1]
    heads = width // head
    chips = n_ctx // 2
    vmem = pl.BlockSpec(memory_space=pltpu.VMEM)
    hbm = pl.BlockSpec(memory_space=pl.ANY)
    dma = pltpu.SemaphoreType.DMA
    sums = []
    for lead in ((4, 4, 4), (4, 4), (4,)):
        for first in (lead, (3,) + lead[1:]):
            for block in ((48, head), (48, head), (16, 2 * head)):
                sums.append(pltpu.VMEM(first + block, BF16))
    return pl.pallas_call(
        functools.partial(backward_kernel, tok * n_ctx),
        out_shape=(
            jax.ShapeDtypeStruct((tok, model), BF16),
            jax.ShapeDtypeStruct((64, 2 * head), F32),
        ),
        in_specs=[vmem] * 5 + [hbm] * 4,
        out_specs=(hbm, vmem),
        scratch_shapes=[
            pltpu.VMEM((n_ctx, tok + 16, 2 * head), BF16),
            pltpu.VMEM((head, heads * tok), BF16),
            pltpu.VMEM((head, heads * tok), BF16),
            pltpu.VMEM((n_ctx, tok, heads * tok), F32),
            pltpu.VMEM((n_ctx, 1, heads * tok), F32),
            pltpu.VMEM((1, heads * tok), F32),
            pltpu.VMEM((1, heads * tok), F32),
            pltpu.VMEM((head, heads * tok), F32),
            pltpu.VMEM((1, heads * tok), F32),
            pltpu.VMEM((head, heads * tok), F32),
            pltpu.VMEM((tok, 2 * head), F32),
            pltpu.VMEM((chips, tok, 2 * head), BF16),
            pltpu.VMEM((chips, tok, 2 * head), BF16),
            pltpu.VMEM((chips, tok, 2 * head), BF16),
            pltpu.VMEM((chips, tok, 2 * head), BF16),
            pltpu.VMEM((tok, model), BF16),
            pltpu.VMEM((model // 128, 2, 64, tok), BF16),
            pltpu.VMEM((model // 128, 64, tok), BF16),
            pltpu.VMEM((model, width), BF16),
            pltpu.VMEM((model, head), BF16),
            pltpu.VMEM((model, head), BF16),
            pltpu.VMEM((tok, width), BF16),
            pltpu.VMEM((2, tok, 2 * head), BF16),
        ] + sums + [
            dma((chips,)), dma((chips,)), dma((n_ctx,)),
            dma((chips,)), dma((chips,)), dma((chips,)), dma((chips,)),
            dma((4,)), dma((model // 512,)), dma((2,)), dma((2,)), dma((3, 3, 3)), dma((3, 3, 3)),
        ],
        compiler_params=pltpu.CompilerParams(
            collective_id=0, has_side_effects=True, vmem_limit_bytes=60 * 1024 * 1024
        ),
    )(queries, key_rows, value_rows, out_grad, doc_ids.reshape(1, -1),
      hidden, q_weight, k_weight, v_weight)


def solution(mesh):
    tokens = P(("dp", "ctx"), None)
    return jax.shard_map(
        functools.partial(on_device, mesh.shape["ctx"]),
        mesh=mesh,
        in_specs=(tokens, tokens, tokens, tokens, tokens, P(("dp", "ctx")), P(), P(), P()),
        out_specs=(tokens, tokens),
        check_vma=False,
    )
```

```python
import functools

import jax
import jax.numpy as jnp
from jax import lax
from jax.experimental import pallas as pl
from jax.experimental.pallas import tpu as pltpu
from jax.sharding import PartitionSpec as P

MESH = pl.DeviceIdType.MESH
BF16 = jnp.bfloat16
F32 = jnp.float32
LOG2E = 1.4426950408889634
MASKED = -1e30


def dot(a, b):
    return jnp.dot(a, b, preferred_element_type=F32)


def dot_rows(a, b):
    return lax.dot_general(a, b, (((1,), (1,)), ((), ())), preferred_element_type=F32)


def backward_kernel(
    seq, q_hbm, k_hbm, v_hbm, do_hbm, docs_hbm, hidden_ref, qw_ref, kw_ref, vw_ref,
    wide, wgrad_ref,
    q_ref, k_ref, v_ref, do_ref, docs_ref, kv, q_t, do_t, probs, max_at, run_max, run_sum, out_t, delta, dq_t, acc,
    pair_out, pair_in, far_out, far_in,
    hidden_t, hidden_in, qw, kw, vw, dq, dkv,
    sum1_x, sum1_y, sum1_z, got1_x, got1_y, got1_z,
    sum2_x, sum2_y, sum2_z, got2_x, got2_y, got2_z,
    sum3_x, sum3_y, sum3_z, got3_x, got3_y, got3_z,
    kv_send, kv_relay, kv_recv, pair_send, pair_recv, far_send, far_recv,
    load_sem, core_send, core_recv, ring_send, ring_recv,
):
    tok, head = k_ref.shape
    heads = q_ref.shape[1] // head
    chips = kv.shape[0] // 2
    scale = head ** -0.5
    row = lax.axis_index("dp")
    me = lax.axis_index("ctx")
    chip, core = me // 2, me % 2
    other = 1 - core
    partner = chip * 2 + other
    place = (row % 4, (chip % 2) * 2 + row // 4, chip // 2)

    def at(ctx):
        return (row, ctx)

    def along(axis, step):
        x, y, z = [lax.rem(p + step, 4) if i == axis else p for i, p in enumerate(place)]
        return ((y % 2) * 4 + x, z * 4 + (y // 2) * 2 + core)

    barrier = pltpu.get_barrier_semaphore()
    for step in range(1, chips):
        peer = lax.rem(chip + step, chips) * 2 + core
        pl.semaphore_signal(barrier, inc=1, device_id=at(peer), device_id_type=MESH)
    pl.semaphore_signal(barrier, inc=1, device_id=at(partner), device_id_type=MESH)
    for axis, step in ((0, 1), (0, 2), (0, 3), (1, 1), (1, 3)):
        pl.semaphore_signal(barrier, inc=1, device_id=along(axis, step), device_id_type=MESH)

    loads = [
        pltpu.make_async_copy(src, dst, load_sem.at[i])
        for i, (src, dst) in enumerate((
            (k_hbm, k_ref), (v_hbm, v_ref), (docs_hbm, docs_ref), (q_hbm, q_ref), (do_hbm, do_ref),
            (hidden_ref, wide), (qw_ref, qw), (kw_ref, kw), (vw_ref, vw)))
    ]
    for load in loads:
        load.start()
    for load in loads[:3]:
        load.wait()

    kv[me, 0:tok, 0:head] = k_ref[...]
    kv[me, 0:tok, head : 2 * head] = v_ref[...]
    last = docs_ref[...] - row * seq
    high, low = last // 64, last % 64
    digit = lax.broadcasted_iota(jnp.int32, (16, tok), 0)
    kv[me, tok : tok + 16, :] = jnp.where(digit == 0, high, low).astype(F32).astype(BF16)
    own_docs = last.astype(F32)

    def kv_copy(slot, send_sem, target):
        return pltpu.make_async_remote_copy(
            src_ref=kv.at[slot], dst_ref=kv.at[slot], send_sem=send_sem,
            recv_sem=kv_recv.at[slot], device_id=at(target), device_id_type=MESH)

    def pair_copy(index):
        return pltpu.make_async_remote_copy(
            src_ref=pair_out.at[index], dst_ref=pair_in.at[index], send_sem=pair_send.at[index],
            recv_sem=pair_recv.at[index], device_id=at(partner), device_id_type=MESH)

    def far_copy(index, slot):
        return pltpu.make_async_remote_copy(
            src_ref=far_out.at[index], dst_ref=far_in.at[slot], send_sem=far_send.at[index],
            recv_sem=far_recv.at[slot], device_id=at(index * 2 + core), device_id_type=MESH)

    for load in loads[3:5]:
        load.wait()
    for h in range(heads):
        cols = slice(h * head, (h + 1) * head)
        rows = slice(h * tok, (h + 1) * tok)
        q_t[:, rows] = q_ref[:, cols].T
        do_t[:, rows] = do_ref[:, cols].T
    pl.semaphore_wait(barrier, chips + 5)

    @pl.when(core == 0)
    def _():
        kv_copy(me, kv_send.at[chip], partner).start()

    @pl.loop(0, chips - 1 - chip)
    def _(i):
        target = chips - 1 - i
        kv_copy(me, kv_send.at[target], target * 2 + core).start()

    run_max[...] = jnp.full_like(run_max, MASKED)
    run_sum[...] = jnp.zeros_like(run_sum)
    out_t[...] = jnp.zeros_like(out_t)
    dq_t[...] = jnp.zeros_like(dq_t)

    loads[5].wait()

    @pl.loop(0, hidden_t.shape[0])
    def _(group):
        turned = wide[:, pl.ds(pl.multiple_of(group * 128, 128), 128)].T
        hidden_t[group, 0] = turned[0:64]
        hidden_t[group, 1] = turned[64:128]

    hidden_copy = pltpu.make_async_remote_copy(
        src_ref=hidden_t.at[:, other], dst_ref=hidden_in, send_sem=core_send.at[0],
        recv_sem=core_recv.at[0], device_id=at(partner), device_id_type=MESH)
    hidden_copy.start()

    @pl.loop(0, 2 * (chip + 1))
    def _(i):
        back, second = i // 2, i % 2
        source = chip - back
        source = jnp.where((chip >= 6) & (source < 4), (source + 2) % 4, source)
        slot = 2 * source + jnp.where(second == 0, core, other)
        skipped = (i == 1) & (core == 0)

        @pl.when((i > 0) & jnp.logical_not(skipped))
        def _():
            kv_copy(slot, kv_relay.at[source], partner).wait_recv()

        @pl.when((i > 0) & (second == 0))
        def _():
            kv_copy(slot, kv_relay.at[source], partner).start()

        @pl.when(jnp.logical_not(skipped))
        def _():
            keys = kv[slot, 0:tok, 0:head]
            values_t = kv[slot, 0:tok, head : 2 * head].T
            digits = kv[slot, tok : tok + 16, :].astype(F32)
            key_docs = digits[0:1, :] * 64.0 + digits[1:2, :]
            key_docs = jnp.broadcast_to(key_docs, (tok, tok)).T
            key_pos = lax.broadcasted_iota(jnp.int32, (tok, tok), 0)
            query_pos = lax.broadcasted_iota(jnp.int32, (tok, tok), 1)
            allowed = (key_docs == own_docs) & (key_pos - query_pos <= (me - slot) * tok)
            for h in range(heads):
                rows = slice(h * tok, (h + 1) * tok)
                scores = dot(keys, q_t[:, rows]) * (scale * LOG2E)
                scores = jnp.where(allowed, scores, MASKED)
                old_max = run_max[:, rows]
                new_max = jnp.maximum(old_max, jnp.max(scores, axis=0, keepdims=True))
                weights = jnp.exp2(scores - new_max)
                shrink = jnp.exp2(old_max - new_max)
                run_max[:, rows] = new_max
                max_at[slot, :, rows] = new_max
                run_sum[:, rows] = run_sum[:, rows] * shrink + jnp.sum(weights, axis=0, keepdims=True)
                probs[slot, :, rows] = weights
                out_t[:, rows] = out_t[:, rows] * shrink + dot(values_t, weights.astype(BF16))

    run_sum[...] = 1.0 / run_sum[...]
    delta[...] = run_sum[...] * jnp.sum(out_t[...] * do_t[...].astype(F32), axis=0, keepdims=True)

    @pl.loop(0, 2 * (chip + 1))
    def _(i):
        source, second = i // 2, i % 2
        slot = 2 * source + jnp.where(second == 0, other, core)
        own_chip = source == chip
        skipped = own_chip & (second == 0) & (core == 0)

        @pl.when(jnp.logical_not(skipped))
        def _():
            keys_t = kv[slot, 0:tok, 0:head].T
            values = kv[slot, 0:tok, head : 2 * head]
            key_part = jnp.zeros((tok, head), F32)
            value_part = jnp.zeros((tok, head), F32)
            for h in range(heads):
                cols = slice(h * head, (h + 1) * head)
                rows = slice(h * tok, (h + 1) * tok)
                factor = jnp.exp2(max_at[slot, :, rows] - run_max[:, rows]) * run_sum[:, rows]
                prob = probs[slot, :, rows] * factor
                prob_grad = dot(values, do_t[:, rows])
                score_grad = (scale * prob * (prob_grad - delta[:, rows])).astype(BF16)
                value_part += dot(prob.astype(BF16), do_ref[:, cols])
                key_part += dot(score_grad, q_ref[:, cols])
                dq_t[:, rows] += dot(keys_t, score_grad)
            acc[:, 0:head] = key_part
            acc[:, head : 2 * head] = value_part

        @pl.when((second == 0) & jnp.logical_not(skipped))
        def _():
            pair_out[source] = acc[...].astype(BF16)
            pair_copy(source).start()

        @pl.when((second == 1) & jnp.logical_not(own_chip))
        def _():
            pair_copy(source).wait_recv()
            far_out[source] = (acc[...] + pair_in[source].astype(F32)).astype(BF16)
            far_copy(source, chip).start()

    for h in range(heads):
        cols = slice(h * head, (h + 1) * head)
        rows = slice(h * tok, (h + 1) * tok)
        dq[:, cols] = dq_t[:, rows].T.astype(BF16)

    @pl.when(core == 0)
    def _():
        pair_copy(chip).wait_recv()
        acc[...] += pair_in[chip].astype(F32)

    @pl.loop(chip + 1, chips)
    def _(source):
        far_copy(source, source).wait_recv()
        acc[...] += far_in[source].astype(F32)

    dkv[0] = acc[...].astype(BF16)
    dkv_copy = pltpu.make_async_remote_copy(
        src_ref=dkv.at[0], dst_ref=dkv.at[1], send_sem=core_send.at[1],
        recv_sem=core_recv.at[1], device_id=at(partner), device_id_type=MESH)
    dkv_copy.start()

    orders = ((0, 1, 2), (1, 2, 0), (2, 0, 1))
    sums = ((sum1_x, sum1_y, sum1_z), (sum2_x, sum2_y, sum2_z), (sum3_x, sum3_y, sum3_z))
    gots = ((got1_x, got1_y, got1_z), (got2_x, got2_y, got2_z), (got3_x, got3_y, got3_z))

    def ring_copy(stage, part, step):
        axis = orders[part][stage]
        return pltpu.make_async_remote_copy(
            src_ref=sums[stage][part].at[lax.rem(place[axis] + step, 4)],
            dst_ref=gots[stage][part].at[step - 1],
            send_sem=ring_send.at[stage, part, step - 1],
            recv_sem=ring_recv.at[stage, part, step - 1],
            device_id=along(axis, step), device_id_type=MESH)

    hidden_copy.wait_recv()
    dkv_copy.wait_recv()
    for step in (2, 1, 3, 0):
        x = lax.rem(place[0] + step, 4)
        for y_lo in range(2):
            groups = pl.ds(y_lo * 32 + x * 8, 8)
            own = hidden_t[groups, core].reshape(512, tok)
            paired = hidden_in[groups].reshape(512, tok)
            terms = (dot(own, dkv[0]) + dot(paired, dkv[1])).astype(BF16).reshape(4, 2, 64, 2 * head)
            for y_hi in range(2):
                y = y_hi * 2 + y_lo
                sum1_x[x, y] = terms[:, y_hi, 0:48, 0:head]
                sum1_y[y, :, x] = terms[:, y_hi, 0:48, head : 2 * head]
                sum1_z[:, x, y] = terms[:, y_hi, 48:64, :]
        if step > 0:
            ring_copy(0, 0, step).start()
    for part in (1, 2):
        for step in (2, 1, 3):
            ring_copy(0, part, step).start()

    for load in loads[6:]:
        load.wait()
    tile = 512

    @pl.loop(0, wide.shape[1] // tile)
    def _(index):
        rows = pl.ds(pl.multiple_of(index * tile, tile), tile)
        total = dot_rows(dq[...], qw[rows, :])
        total += dot_rows(dkv[0, :, 0:head], kw[rows, :])
        total += dot_rows(dkv[0, :, head : 2 * head], vw[rows, :])
        wide[:, rows] = total.astype(BF16)

    for stage in range(3):
        for part in range(3):
            for step in (1, 3, 2):
                ring_copy(stage, part, step).wait_recv()
            mine = place[orders[part][stage]]
            total = sums[stage][part][mine].astype(F32)
            for step in range(3):
                total += gots[stage][part][step].astype(F32)
            if stage < 2:
                sums[stage + 1][part][...] = total.astype(sums[stage + 1][part].dtype)
                for step in (2, 1, 3):
                    ring_copy(stage + 1, part, step).start()
            else:
                wgrad_ref[(slice(0, 48), slice(0, 48), slice(48, 64))[part],
                          (slice(0, head), slice(head, 2 * head), slice(0, 2 * head))[part]] = total

    hidden_copy.wait_send()
    dkv_copy.wait_send()
    for stage in range(3):
        for part in range(3):
            for step in (1, 2, 3):
                ring_copy(stage, part, step).wait_send()

    @pl.when(core == 0)
    def _():
        kv_copy(me, kv_send.at[chip], partner).wait_send()

    @pl.when(core == 1)
    def _():
        pair_copy(chip).wait_send()

    @pl.loop(chip + 1, chips)
    def _(target):
        kv_copy(me, kv_send.at[target], target * 2 + core).wait_send()

    @pl.loop(0, chip)
    def _(source):
        kv_copy(2 * source + core, kv_relay.at[source], partner).wait_send()
        pair_copy(source).wait_send()
        far_copy(source, chip).wait_send()


def finish_kernel(grad_ref, wgrad_ref, grad_out, wgrad_out, sem):
    copies = [
        pltpu.make_async_copy(grad_ref, grad_out, sem.at[0]),
        pltpu.make_async_copy(wgrad_ref, wgrad_out, sem.at[1]),
    ]
    for copy in copies:
        copy.start()
    for copy in copies:
        copy.wait()


def on_device(
    n_ctx, hidden, queries, key_rows, value_rows, out_grad, doc_ids, q_weight, k_weight, v_weight
):
    tok, head = key_rows.shape
    width = queries.shape[1]
    model = hidden.shape[1]
    heads = width // head
    chips = n_ctx // 2
    vmem = pl.BlockSpec(memory_space=pltpu.VMEM)
    hbm = pl.BlockSpec(memory_space=pl.ANY)
    dma = pltpu.SemaphoreType.DMA
    sums = []
    for lead in ((4, 4, 4), (4, 4), (4,)):
        for first in (lead, (3,) + lead[1:]):
            for block in ((48, head), (48, head), (16, 2 * head)):
                sums.append(pltpu.VMEM(first + block, BF16))
    grads = pl.pallas_call(
        functools.partial(backward_kernel, tok * n_ctx),
        out_shape=(pltpu.VMEM((tok, model), BF16), pltpu.VMEM((64, 2 * head), F32)),
        in_specs=[hbm] * 9,
        out_specs=(vmem, vmem),
        scratch_shapes=[
            pltpu.VMEM((tok, width), BF16),
            pltpu.VMEM((tok, head), BF16),
            pltpu.VMEM((tok, head), BF16),
            pltpu.VMEM((tok, width), BF16),
            pltpu.VMEM((1, tok), jnp.int32),
            pltpu.VMEM((n_ctx, tok + 16, 2 * head), BF16),
            pltpu.VMEM((head, heads * tok), BF16),
            pltpu.VMEM((head, heads * tok), BF16),
            pltpu.VMEM((n_ctx, tok, heads * tok), F32),
            pltpu.VMEM((n_ctx, 1, heads * tok), F32),
            pltpu.VMEM((1, heads * tok), F32),
            pltpu.VMEM((1, heads * tok), F32),
            pltpu.VMEM((head, heads * tok), F32),
            pltpu.VMEM((1, heads * tok), F32),
            pltpu.VMEM((head, heads * tok), F32),
            pltpu.VMEM((tok, 2 * head), F32),
            pltpu.VMEM((chips, tok, 2 * head), BF16),
            pltpu.VMEM((chips, tok, 2 * head), BF16),
            pltpu.VMEM((chips, tok, 2 * head), BF16),
            pltpu.VMEM((chips, tok, 2 * head), BF16),
            pltpu.VMEM((model // 128, 2, 64, tok), BF16),
            pltpu.VMEM((model // 128, 64, tok), BF16),
            pltpu.VMEM((model, width), BF16),
            pltpu.VMEM((model, head), BF16),
            pltpu.VMEM((model, head), BF16),
            pltpu.VMEM((tok, width), BF16),
            pltpu.VMEM((2, tok, 2 * head), BF16),
        ] + sums + [
            dma((chips,)), dma((chips,)), dma((n_ctx,)),
            dma((chips,)), dma((chips,)), dma((chips,)), dma((chips,)),
            dma((9,)), dma((2,)), dma((2,)), dma((3, 3, 3)), dma((3, 3, 3)),
        ],
        compiler_params=pltpu.CompilerParams(
            collective_id=0, has_side_effects=True, vmem_limit_bytes=56 * 1024 * 1024
        ),
    )(queries, key_rows, value_rows, out_grad, doc_ids.reshape(1, -1),
      hidden, q_weight, k_weight, v_weight)
    return pl.pallas_call(
        finish_kernel,
        out_shape=(
            jax.ShapeDtypeStruct((tok, model), BF16),
            jax.ShapeDtypeStruct((64, 2 * head), F32),
        ),
        in_specs=[vmem] * 2,
        out_specs=(hbm, hbm),
        scratch_shapes=[dma((2,))],
        compiler_params=pltpu.CompilerParams(vmem_limit_bytes=4 * 1024 * 1024),
    )(*grads)


def solution(mesh):
    tokens = P(("dp", "ctx"), None)
    return jax.shard_map(
        functools.partial(on_device, mesh.shape["ctx"]),
        mesh=mesh,
        in_specs=(tokens, tokens, tokens, tokens, tokens, P(("dp", "ctx")), P(), P(), P()),
        out_specs=(tokens, tokens),
        check_vma=False,
    )
```

```python
import functools

import jax
import jax.numpy as jnp
from jax import lax
from jax.experimental import pallas as pl
from jax.experimental.pallas import tpu as pltpu
from jax.sharding import PartitionSpec as P

MESH = pl.DeviceIdType.MESH
BF16 = jnp.bfloat16
F32 = jnp.float32
LOG2E = 1.4426950408889634
MASKED = -1e30


def dot(a, b):
    return jnp.dot(a, b, preferred_element_type=F32)


def dot_rows(a, b):
    return lax.dot_general(a, b, (((1,), (1,)), ((), ())), preferred_element_type=F32)


def backward_kernel(
    seq, q_hbm, k_hbm, v_hbm, do_hbm, docs_hbm, hidden_ref, qw_ref, kw_ref, vw_ref,
    wide, wgrad_ref,
    q_ref, k_ref, v_ref, do_ref, docs_ref, kv, q_t, do_t, probs, max_at, run_max, run_sum, score_grads, delta, dq_t, acc,
    pair_out, pair_in, far_out, far_in,
    hidden_t, hidden_in, qw, kw, vw, dq, dkv,
    sum1_x, sum1_y, sum1_z, got1_x, got1_y, got1_z,
    sum2_x, sum2_y, sum2_z, got2_x, got2_y, got2_z,
    sum3_x, sum3_y, sum3_z, got3_x, got3_y, got3_z,
    kv_send, kv_relay, kv_recv, pair_send, pair_recv, far_send, far_recv,
    load_sem, core_send, core_recv, ring_send, ring_recv,
):
    tok, head = k_ref.shape
    heads = q_ref.shape[1] // head
    chips = kv.shape[0] // 2
    scale = head ** -0.5
    row = lax.axis_index("dp")
    me = lax.axis_index("ctx")
    chip, core = me // 2, me % 2
    other = 1 - core
    partner = chip * 2 + other
    place = (row % 4, (chip % 2) * 2 + row // 4, chip // 2)

    def at(ctx):
        return (row, ctx)

    def along(axis, step):
        x, y, z = [lax.rem(p + step, 4) if i == axis else p for i, p in enumerate(place)]
        return ((y % 2) * 4 + x, z * 4 + (y // 2) * 2 + core)

    barrier = pltpu.get_barrier_semaphore()
    for step in range(1, chips):
        peer = lax.rem(chip + step, chips) * 2 + core
        pl.semaphore_signal(barrier, inc=1, device_id=at(peer), device_id_type=MESH)
    pl.semaphore_signal(barrier, inc=1, device_id=at(partner), device_id_type=MESH)
    for axis, step in ((0, 1), (0, 2), (0, 3), (1, 1), (1, 3)):
        pl.semaphore_signal(barrier, inc=1, device_id=along(axis, step), device_id_type=MESH)

    loads = [
        pltpu.make_async_copy(src, dst, load_sem.at[i])
        for i, (src, dst) in enumerate((
            (k_hbm, k_ref), (v_hbm, v_ref), (docs_hbm, docs_ref), (q_hbm, q_ref), (do_hbm, do_ref),
            (hidden_ref, wide), (qw_ref, qw), (kw_ref, kw), (vw_ref, vw)))
    ]
    for load in loads:
        load.start()
    for load in loads[:3]:
        load.wait()

    kv[me, 0:tok, 0:head] = k_ref[...]
    kv[me, 0:tok, head : 2 * head] = v_ref[...]
    last = docs_ref[...] - row * seq
    high, low = last // 64, last % 64
    digit = lax.broadcasted_iota(jnp.int32, (16, tok), 0)
    kv[me, tok : tok + 16, :] = jnp.where(digit == 0, high, low).astype(F32).astype(BF16)
    own_docs = last.astype(F32)

    def kv_copy(slot, send_sem, target):
        return pltpu.make_async_remote_copy(
            src_ref=kv.at[slot], dst_ref=kv.at[slot], send_sem=send_sem,
            recv_sem=kv_recv.at[slot], device_id=at(target), device_id_type=MESH)

    def pair_copy(index):
        return pltpu.make_async_remote_copy(
            src_ref=pair_out.at[index], dst_ref=pair_in.at[index], send_sem=pair_send.at[index],
            recv_sem=pair_recv.at[index], device_id=at(partner), device_id_type=MESH)

    def far_copy(index, slot):
        return pltpu.make_async_remote_copy(
            src_ref=far_out.at[index], dst_ref=far_in.at[slot], send_sem=far_send.at[index],
            recv_sem=far_recv.at[slot], device_id=at(index * 2 + core), device_id_type=MESH)

    for load in loads[3:5]:
        load.wait()
    for h in range(heads):
        cols = slice(h * head, (h + 1) * head)
        rows = slice(h * tok, (h + 1) * tok)
        q_t[:, rows] = q_ref[:, cols].T
        do_t[:, rows] = do_ref[:, cols].T
    pl.semaphore_wait(barrier, chips + 5)

    @pl.when(core == 0)
    def _():
        kv_copy(me, kv_send.at[chip], partner).start()

    @pl.loop(0, chips - 1 - chip)
    def _(i):
        target = chips - 1 - i
        kv_copy(me, kv_send.at[target], target * 2 + core).start()

    run_max[...] = jnp.full_like(run_max, MASKED)
    run_sum[...] = jnp.zeros_like(run_sum)
    delta[...] = jnp.zeros_like(delta)
    dq_t[...] = jnp.zeros_like(dq_t)

    pieces = 16
    piece_groups = hidden_t.shape[0] // pieces

    def hidden_copy(piece):
        groups = pl.ds(piece * piece_groups, piece_groups)
        return pltpu.make_async_remote_copy(
            src_ref=hidden_t.at[groups, other], dst_ref=hidden_in.at[groups],
            send_sem=core_send.at[piece], recv_sem=core_recv.at[piece],
            device_id=at(partner), device_id_type=MESH)

    @pl.loop(0, 2 * (chip + 1))
    def _(i):
        back, second = i // 2, i % 2
        source = chip - back
        source = jnp.where((chip >= 6) & (source < 4), (source + 2) % 4, source)
        slot = 2 * source + jnp.where(second == 0, core, other)
        skipped = (i == 1) & (core == 0)

        @pl.when((i > 0) & jnp.logical_not(skipped))
        def _():
            kv_copy(slot, kv_relay.at[source], partner).wait_recv()

        @pl.when((i > 0) & (second == 0))
        def _():
            kv_copy(slot, kv_relay.at[source], partner).start()

        @pl.when(jnp.logical_not(skipped))
        def _():
            keys = kv[slot, 0:tok, 0:head]
            values = kv[slot, 0:tok, head : 2 * head]
            digits = kv[slot, tok : tok + 16, :].astype(F32)
            key_docs = digits[0:1, :] * 64.0 + digits[1:2, :]
            key_docs = jnp.broadcast_to(key_docs, (tok, tok)).T
            key_pos = lax.broadcasted_iota(jnp.int32, (tok, tok), 0)
            query_pos = lax.broadcasted_iota(jnp.int32, (tok, tok), 1)
            allowed = (key_docs == own_docs) & (key_pos - query_pos <= (me - slot) * tok)
            for h in range(heads):
                rows = slice(h * tok, (h + 1) * tok)
                scores = dot(keys, q_t[:, rows]) * (scale * LOG2E)
                scores = jnp.where(allowed, scores, MASKED)
                old_max = run_max[:, rows]
                new_max = jnp.maximum(old_max, jnp.max(scores, axis=0, keepdims=True))
                weights = jnp.exp2(scores - new_max)
                shrink = jnp.exp2(old_max - new_max)
                run_max[:, rows] = new_max
                max_at[slot, :, rows] = new_max
                run_sum[:, rows] = run_sum[:, rows] * shrink + jnp.sum(weights, axis=0, keepdims=True)
                probs[slot, :, rows] = weights
                prob_grad = dot(values, do_t[:, rows])
                delta[:, rows] = delta[:, rows] * shrink + jnp.sum(
                    weights * prob_grad, axis=0, keepdims=True)

        @pl.when(i == 0)
        def _():
            loads[5].wait()

            @pl.loop(0, hidden_t.shape[0])
            def _(group):
                turned = wide[:, pl.ds(pl.multiple_of(group * 128, 128), 128)].T
                hidden_t[group, 0] = turned[0:64]
                hidden_t[group, 1] = turned[64:128]

    run_sum[...] = 1.0 / run_sum[...]
    delta[...] = delta[...] * run_sum[...]

    @pl.loop(0, 2 * (chip + 1))
    def _(i):
        turn, second = i // 2, i % 2
        third = turn % 3
        spread = jnp.where(third == 0, 2, (third - 1) * 4) + turn // 3
        paired = (turn % 2) * 2 + turn // 2
        source = jnp.where((chip >= 6) & (turn < 6), spread,
                           jnp.where((chip // 2 == 2) & (turn < 4), paired, turn))
        slot = 2 * source + jnp.where(second == 0, other, core)
        own_chip = source == chip
        skipped = own_chip & (second == 0) & (core == 0)

        @pl.when(jnp.logical_not(skipped))
        def _():
            keys_t = kv[slot, 0:tok, 0:head].T
            values = kv[slot, 0:tok, head : 2 * head]
            key_part = jnp.zeros((tok, head), F32)
            value_part = jnp.zeros((tok, head), F32)
            for h in range(heads):
                cols = slice(h * head, (h + 1) * head)
                rows = slice(h * tok, (h + 1) * tok)
                factor = jnp.exp2(max_at[slot, :, rows] - run_max[:, rows]) * run_sum[:, rows]
                prob = probs[slot, :, rows] * factor
                prob_grad = dot(values, do_t[:, rows])
                score_grad = (scale * prob * (prob_grad - delta[:, rows])).astype(BF16)
                value_part += dot(prob.astype(BF16), do_ref[:, cols])
                key_part += dot(score_grad, q_ref[:, cols])
                score_grads[:, rows] = score_grad
            dq_t[...] += dot(keys_t, score_grads[...])
            acc[:, 0:head] = key_part
            acc[:, head : 2 * head] = value_part

        @pl.when((second == 0) & jnp.logical_not(skipped))
        def _():
            pair_out[source] = acc[...].astype(BF16)
            pair_copy(source).start()

        @pl.when((second == 1) & jnp.logical_not(own_chip))
        def _():
            pair_copy(source).wait_recv()
            far_out[source] = (acc[...] + pair_in[source].astype(F32)).astype(BF16)
            far_copy(source, chip).start()

        hidden_copy(i).start()

    @pl.loop(2 * (chip + 1), pieces)
    def _(piece):
        hidden_copy(piece).start()

    for h in range(heads):
        cols = slice(h * head, (h + 1) * head)
        rows = slice(h * tok, (h + 1) * tok)
        dq[:, cols] = dq_t[:, rows].T.astype(BF16)

    @pl.when(core == 0)
    def _():
        pair_copy(chip).wait_recv()
        acc[...] += pair_in[chip].astype(F32)

    @pl.loop(chip + 1, chips)
    def _(source):
        far_copy(source, source).wait_recv()
        acc[...] += far_in[source].astype(F32)

    dkv[0] = acc[...].astype(BF16)
    dkv_copy = pltpu.make_async_remote_copy(
        src_ref=dkv.at[0], dst_ref=dkv.at[1], send_sem=core_send.at[pieces],
        recv_sem=core_recv.at[pieces], device_id=at(partner), device_id_type=MESH)
    dkv_copy.start()

    orders = ((0, 1, 2), (1, 2, 0), (2, 0, 1))
    sums = ((sum1_x, sum1_y, sum1_z), (sum2_x, sum2_y, sum2_z), (sum3_x, sum3_y, sum3_z))
    gots = ((got1_x, got1_y, got1_z), (got2_x, got2_y, got2_z), (got3_x, got3_y, got3_z))

    def ring_copy(stage, part, step):
        axis = orders[part][stage]
        return pltpu.make_async_remote_copy(
            src_ref=sums[stage][part].at[lax.rem(place[axis] + step, 4)],
            dst_ref=gots[stage][part].at[step - 1],
            send_sem=ring_send.at[stage, part, step - 1],
            recv_sem=ring_recv.at[stage, part, step - 1],
            device_id=along(axis, step), device_id_type=MESH)

    @pl.loop(0, pieces)
    def _(piece):
        hidden_copy(piece).wait_recv()

    dkv_copy.wait_recv()
    for step in (2, 1, 3, 0):
        x = lax.rem(place[0] + step, 4)
        for y_lo in range(2):
            groups = pl.ds(y_lo * 32 + x * 8, 8)
            own = hidden_t[groups, core].reshape(512, tok)
            paired = hidden_in[groups].reshape(512, tok)
            terms = (dot(own, dkv[0]) + dot(paired, dkv[1])).astype(BF16).reshape(4, 2, 64, 2 * head)
            for y_hi in range(2):
                y = y_hi * 2 + y_lo
                sum1_x[x, y] = terms[:, y_hi, 0:48, 0:head]
                sum1_y[y, :, x] = terms[:, y_hi, 0:48, head : 2 * head]
                sum1_z[:, x, y] = terms[:, y_hi, 48:64, :]
        if step > 0:
            ring_copy(0, 0, step).start()
    for part in (1, 2):
        for step in (2, 1, 3):
            ring_copy(0, part, step).start()

    for load in loads[6:]:
        load.wait()
    tile = 512

    @pl.loop(0, wide.shape[1] // tile)
    def _(index):
        rows = pl.ds(pl.multiple_of(index * tile, tile), tile)
        total = dot_rows(dq[...], qw[rows, :])
        total += dot_rows(dkv[0, :, 0:head], kw[rows, :])
        total += dot_rows(dkv[0, :, head : 2 * head], vw[rows, :])
        wide[:, rows] = total.astype(BF16)

    for stage in range(3):
        for part in range(3):
            for step in (1, 3, 2):
                ring_copy(stage, part, step).wait_recv()
            mine = place[orders[part][stage]]
            total = sums[stage][part][mine].astype(F32)
            for step in range(3):
                total += gots[stage][part][step].astype(F32)
            if stage < 2:
                sums[stage + 1][part][...] = total.astype(sums[stage + 1][part].dtype)
                for step in (2, 1, 3):
                    ring_copy(stage + 1, part, step).start()
            else:
                wgrad_ref[(slice(0, 48), slice(0, 48), slice(48, 64))[part],
                          (slice(0, head), slice(head, 2 * head), slice(0, 2 * head))[part]] = total

    @pl.loop(0, pieces)
    def _(piece):
        hidden_copy(piece).wait_send()

    dkv_copy.wait_send()
    for stage in range(3):
        for part in range(3):
            for step in (1, 2, 3):
                ring_copy(stage, part, step).wait_send()

    @pl.when(core == 0)
    def _():
        kv_copy(me, kv_send.at[chip], partner).wait_send()

    @pl.when(core == 1)
    def _():
        pair_copy(chip).wait_send()

    @pl.loop(chip + 1, chips)
    def _(target):
        kv_copy(me, kv_send.at[target], target * 2 + core).wait_send()

    @pl.loop(0, chip)
    def _(source):
        kv_copy(2 * source + core, kv_relay.at[source], partner).wait_send()
        pair_copy(source).wait_send()
        far_copy(source, chip).wait_send()


def finish_kernel(grad_ref, wgrad_ref, grad_out, wgrad_out, sem):
    copies = [
        pltpu.make_async_copy(grad_ref, grad_out, sem.at[0]),
        pltpu.make_async_copy(wgrad_ref, wgrad_out, sem.at[1]),
    ]
    for copy in copies:
        copy.start()
    for copy in copies:
        copy.wait()


def on_device(
    n_ctx, hidden, queries, key_rows, value_rows, out_grad, doc_ids, q_weight, k_weight, v_weight
):
    tok, head = key_rows.shape
    width = queries.shape[1]
    model = hidden.shape[1]
    heads = width // head
    chips = n_ctx // 2
    vmem = pl.BlockSpec(memory_space=pltpu.VMEM)
    hbm = pl.BlockSpec(memory_space=pl.ANY)
    dma = pltpu.SemaphoreType.DMA
    sums = []
    for lead in ((4, 4, 4), (4, 4), (4,)):
        for first in (lead, (3,) + lead[1:]):
            for block in ((48, head), (48, head), (16, 2 * head)):
                sums.append(pltpu.VMEM(first + block, BF16))
    grads = pl.pallas_call(
        functools.partial(backward_kernel, tok * n_ctx),
        out_shape=(pltpu.VMEM((tok, model), BF16), pltpu.VMEM((64, 2 * head), F32)),
        in_specs=[hbm] * 9,
        out_specs=(vmem, vmem),
        scratch_shapes=[
            pltpu.VMEM((tok, width), BF16),
            pltpu.VMEM((tok, head), BF16),
            pltpu.VMEM((tok, head), BF16),
            pltpu.VMEM((tok, width), BF16),
            pltpu.VMEM((1, tok), jnp.int32),
            pltpu.VMEM((n_ctx, tok + 16, 2 * head), BF16),
            pltpu.VMEM((head, heads * tok), BF16),
            pltpu.VMEM((head, heads * tok), BF16),
            pltpu.VMEM((n_ctx, tok, heads * tok), F32),
            pltpu.VMEM((n_ctx, 1, heads * tok), F32),
            pltpu.VMEM((1, heads * tok), F32),
            pltpu.VMEM((1, heads * tok), F32),
            pltpu.VMEM((tok, heads * tok), BF16),
            pltpu.VMEM((1, heads * tok), F32),
            pltpu.VMEM((head, heads * tok), F32),
            pltpu.VMEM((tok, 2 * head), F32),
            pltpu.VMEM((chips, tok, 2 * head), BF16),
            pltpu.VMEM((chips, tok, 2 * head), BF16),
            pltpu.VMEM((chips, tok, 2 * head), BF16),
            pltpu.VMEM((chips, tok, 2 * head), BF16),
            pltpu.VMEM((model // 128, 2, 64, tok), BF16),
            pltpu.VMEM((model // 128, 64, tok), BF16),
            pltpu.VMEM((model, width), BF16),
            pltpu.VMEM((model, head), BF16),
            pltpu.VMEM((model, head), BF16),
            pltpu.VMEM((tok, width), BF16),
            pltpu.VMEM((2, tok, 2 * head), BF16),
        ] + sums + [
            dma((chips,)), dma((chips,)), dma((n_ctx,)),
            dma((chips,)), dma((chips,)), dma((chips,)), dma((chips,)),
            dma((9,)), dma((17,)), dma((17,)), dma((3, 3, 3)), dma((3, 3, 3)),
        ],
        compiler_params=pltpu.CompilerParams(
            collective_id=0, has_side_effects=True, vmem_limit_bytes=56 * 1024 * 1024
        ),
    )(queries, key_rows, value_rows, out_grad, doc_ids.reshape(1, -1),
      hidden, q_weight, k_weight, v_weight)
    return pl.pallas_call(
        finish_kernel,
        out_shape=(
            jax.ShapeDtypeStruct((tok, model), BF16),
            jax.ShapeDtypeStruct((64, 2 * head), F32),
        ),
        in_specs=[vmem] * 2,
        out_specs=(hbm, hbm),
        scratch_shapes=[dma((2,))],
        compiler_params=pltpu.CompilerParams(vmem_limit_bytes=4 * 1024 * 1024),
    )(*grads)


def solution(mesh):
    tokens = P(("dp", "ctx"), None)
    return jax.shard_map(
        functools.partial(on_device, mesh.shape["ctx"]),
        mesh=mesh,
        in_specs=(tokens, tokens, tokens, tokens, tokens, P(("dp", "ctx")), P(), P(), P()),
        out_specs=(tokens, tokens),
        check_vma=False,
    )
```

```python
import functools

import jax
import jax.numpy as jnp
from jax import lax
from jax.experimental import pallas as pl
from jax.experimental.pallas import tpu as pltpu
from jax.sharding import PartitionSpec as P

MESH = pl.DeviceIdType.MESH
BF16 = jnp.bfloat16
F32 = jnp.float32
LOG2E = 1.4426950408889634
MASKED = -1e30


def dot(a, b):
    return jnp.dot(a, b, preferred_element_type=F32)


def dot_rows(a, b):
    return lax.dot_general(a, b, (((1,), (1,)), ((), ())), preferred_element_type=F32)


def backward_kernel(
    seq, q_hbm, k_hbm, v_hbm, do_hbm, docs_hbm, hidden_ref, qw_ref, kw_ref, vw_ref,
    wide, wgrad_ref,
    q_ref, k_ref, v_ref, do_ref, docs_ref, kv, q_t, do_t, probs, max_at, run_max, run_sum, score_grads, delta, dq_t, parts,
    pair_out, pair_in, far_out, far_in,
    hidden_t, hidden_in, qw, kw, vw, dq, dkv,
    sum1_x, sum1_y, sum1_z, got1_x, got1_y, got1_z,
    sum2_x, sum2_y, sum2_z, got2_x, got2_y, got2_z,
    sum3_x, sum3_y, sum3_z, got3_x, got3_y, got3_z,
    kv_send, kv_relay, kv_recv, pair_send, pair_recv, far_send, far_recv,
    load_sem, core_send, core_recv, ring_send, ring_recv,
):
    tok, head = k_ref.shape
    heads = q_ref.shape[1] // head
    chips = kv.shape[0] // 2
    scale = head ** -0.5
    row = lax.axis_index("dp")
    me = lax.axis_index("ctx")
    chip, core = me // 2, me % 2
    other = 1 - core
    partner = chip * 2 + other
    place = (row % 4, (chip % 2) * 2 + row // 4, chip // 2)

    def at(ctx):
        return (row, ctx)

    def along(axis, step):
        x, y, z = [lax.rem(p + step, 4) if i == axis else p for i, p in enumerate(place)]
        return ((y % 2) * 4 + x, z * 4 + (y // 2) * 2 + core)

    barrier = pltpu.get_barrier_semaphore()
    for step in range(1, chips):
        peer = lax.rem(chip + step, chips) * 2 + core
        pl.semaphore_signal(barrier, inc=1, device_id=at(peer), device_id_type=MESH)
    pl.semaphore_signal(barrier, inc=1, device_id=at(partner), device_id_type=MESH)
    for axis, step in ((0, 1), (0, 2), (0, 3), (1, 1), (1, 3)):
        pl.semaphore_signal(barrier, inc=1, device_id=along(axis, step), device_id_type=MESH)

    loads = [
        pltpu.make_async_copy(src, dst, load_sem.at[i])
        for i, (src, dst) in enumerate((
            (k_hbm, k_ref), (v_hbm, v_ref), (docs_hbm, docs_ref), (q_hbm, q_ref), (do_hbm, do_ref),
            (hidden_ref, wide), (qw_ref, qw), (kw_ref, kw), (vw_ref, vw)))
    ]
    for load in loads:
        load.start()
    for load in loads[:3]:
        load.wait()

    kv[me, 0:tok, 0:head] = k_ref[...]
    kv[me, 0:tok, head : 2 * head] = v_ref[...]
    last = docs_ref[...] - row * seq
    high, low = last // 64, last % 64
    digit = lax.broadcasted_iota(jnp.int32, (16, tok), 0)
    kv[me, tok : tok + 16, :] = jnp.where(digit == 0, high, low).astype(F32).astype(BF16)
    own_docs = last.astype(F32)

    def kv_copy(slot, send_sem, target):
        return pltpu.make_async_remote_copy(
            src_ref=kv.at[slot], dst_ref=kv.at[slot], send_sem=send_sem,
            recv_sem=kv_recv.at[slot], device_id=at(target), device_id_type=MESH)

    def pair_copy(index):
        return pltpu.make_async_remote_copy(
            src_ref=pair_out.at[index], dst_ref=pair_in.at[index], send_sem=pair_send.at[index],
            recv_sem=pair_recv.at[index], device_id=at(partner), device_id_type=MESH)

    def far_copy(index, slot):
        return pltpu.make_async_remote_copy(
            src_ref=far_out.at[index], dst_ref=far_in.at[slot], send_sem=far_send.at[index],
            recv_sem=far_recv.at[slot], device_id=at(index * 2 + core), device_id_type=MESH)

    for load in loads[3:5]:
        load.wait()
    for h in range(heads):
        cols = slice(h * head, (h + 1) * head)
        rows = slice(h * tok, (h + 1) * tok)
        q_t[:, rows] = q_ref[:, cols].T
        do_t[:, rows] = do_ref[:, cols].T
    pl.semaphore_wait(barrier, chips + 5)

    @pl.when(core == 0)
    def _():
        kv_copy(me, kv_send.at[chip], partner).start()

    @pl.loop(0, chips - 1 - chip)
    def _(i):
        target = chips - 1 - i
        kv_copy(me, kv_send.at[target], target * 2 + core).start()

    run_max[...] = jnp.full_like(run_max, MASKED)
    run_sum[...] = jnp.zeros_like(run_sum)
    delta[...] = jnp.zeros_like(delta)
    dq_t[...] = jnp.zeros_like(dq_t)

    pieces = 16
    piece_groups = hidden_t.shape[0] // pieces

    def hidden_copy(piece):
        groups = pl.ds(piece * piece_groups, piece_groups)
        return pltpu.make_async_remote_copy(
            src_ref=hidden_t.at[groups, other], dst_ref=hidden_in.at[groups],
            send_sem=core_send.at[piece], recv_sem=core_recv.at[piece],
            device_id=at(partner), device_id_type=MESH)

    @pl.loop(0, 2 * (chip + 1))
    def _(i):
        last_step = i == 2 * chip + 1
        second = jnp.where(last_step | ((i > 0) & (i % 2 == 0)), 1, 0)
        back = jnp.where(last_step, chip, jnp.where(second == 1, i // 2 - 1, (i + 1) // 2))
        source = chip - back
        source = jnp.where((chip >= 6) & (source < 4), (source + 2) % 4, source)
        slot = 2 * source + jnp.where(second == 0, core, other)
        skipped = (back == 0) & (second == 1) & (core == 0)

        @pl.when((i > 0) & jnp.logical_not(skipped))
        def _():
            kv_copy(slot, kv_relay.at[source], partner).wait_recv()

        @pl.when((i > 0) & (second == 0))
        def _():
            kv_copy(slot, kv_relay.at[source], partner).start()

        @pl.when(jnp.logical_not(skipped))
        def _():
            keys = kv[slot, 0:tok, 0:head]
            values = kv[slot, 0:tok, head : 2 * head]
            digits = kv[slot, tok : tok + 16, :].astype(F32)
            key_docs = digits[0:1, :] * 64.0 + digits[1:2, :]
            key_docs = jnp.broadcast_to(key_docs, (tok, tok)).T
            key_pos = lax.broadcasted_iota(jnp.int32, (tok, tok), 0)
            query_pos = lax.broadcasted_iota(jnp.int32, (tok, tok), 1)
            allowed = (key_docs == own_docs) & (key_pos - query_pos <= (me - slot) * tok)
            for h in range(heads):
                rows = slice(h * tok, (h + 1) * tok)
                scores = dot(keys, q_t[:, rows]) * (scale * LOG2E)
                scores = jnp.where(allowed, scores, MASKED)
                old_max = run_max[:, rows]
                new_max = jnp.maximum(old_max, jnp.max(scores, axis=0, keepdims=True))
                weights = jnp.exp2(scores - new_max)
                shrink = jnp.exp2(old_max - new_max)
                run_max[:, rows] = new_max
                max_at[slot, :, rows] = new_max
                run_sum[:, rows] = run_sum[:, rows] * shrink + jnp.sum(weights, axis=0, keepdims=True)
                probs[slot, :, rows] = weights
                prob_grad = dot(values, do_t[:, rows])
                delta[:, rows] = delta[:, rows] * shrink + jnp.sum(
                    weights * prob_grad, axis=0, keepdims=True)

        @pl.when(i == 0)
        def _():
            loads[5].wait()

            @pl.loop(0, hidden_t.shape[0])
            def _(group):
                turned = wide[:, pl.ds(pl.multiple_of(group * 128, 128), 128)].T
                hidden_t[group, 0] = turned[0:64]
                hidden_t[group, 1] = turned[64:128]

    run_sum[...] = 1.0 / run_sum[...]
    delta[...] = delta[...] * run_sum[...]

    def target_of(turn):
        across = (chip + 1) // 2
        own_side = chip % 2
        return jnp.where(turn == chip, chip, jnp.where(
            turn < across, 2 * turn + 1 - own_side, 2 * (turn - across) + own_side))

    @pl.loop(0, 2 * (chip + 1))
    def _(i):
        turn, second = i // 2, i % 2
        source = target_of(turn)
        slot = 2 * source + jnp.where(second == 0, other, core)
        own_chip = source == chip
        skipped = own_chip & (second == 0) & (core == 0)

        @pl.when(jnp.logical_not(skipped))
        def _():
            keys_t = kv[slot, 0:tok, 0:head].T
            values = kv[slot, 0:tok, head : 2 * head]
            key_part = jnp.zeros((tok, head), F32)
            value_part = jnp.zeros((tok, head), F32)
            for h in range(heads):
                cols = slice(h * head, (h + 1) * head)
                rows = slice(h * tok, (h + 1) * tok)
                factor = jnp.exp2(max_at[slot, :, rows] - run_max[:, rows]) * run_sum[:, rows]
                prob = probs[slot, :, rows] * factor
                prob_grad = dot(values, do_t[:, rows])
                score_grad = (scale * prob * (prob_grad - delta[:, rows])).astype(BF16)
                value_part += dot(prob.astype(BF16), do_ref[:, cols])
                key_part += dot(score_grad, q_ref[:, cols])
                score_grads[:, rows] = score_grad
            dq_t[...] += dot(keys_t, score_grads[...])
            parts[second, :, 0:head] = key_part
            parts[second, :, head : 2 * head] = value_part

        @pl.when((second == 0) & jnp.logical_not(skipped))
        def _():
            pair_out[source] = parts[0].astype(BF16)
            pair_copy(source).start()

        @pl.when((second == 0) & (turn > 0))
        def _():
            before = target_of(turn - 1)
            pair_copy(before).wait_recv()
            far_out[before] = (parts[1] + pair_in[before].astype(F32)).astype(BF16)
            far_copy(before, chip).start()

        hidden_copy(i).start()

    @pl.loop(2 * (chip + 1), pieces)
    def _(piece):
        hidden_copy(piece).start()

    for h in range(heads):
        cols = slice(h * head, (h + 1) * head)
        rows = slice(h * tok, (h + 1) * tok)
        dq[:, cols] = dq_t[:, rows].T.astype(BF16)

    @pl.when(core == 0)
    def _():
        pair_copy(chip).wait_recv()
        parts[1] += pair_in[chip].astype(F32)

    @pl.loop(chip + 1, chips)
    def _(source):
        far_copy(source, source).wait_recv()
        parts[1] += far_in[source].astype(F32)

    dkv[0] = parts[1].astype(BF16)
    dkv_copy = pltpu.make_async_remote_copy(
        src_ref=dkv.at[0], dst_ref=dkv.at[1], send_sem=core_send.at[pieces],
        recv_sem=core_recv.at[pieces], device_id=at(partner), device_id_type=MESH)
    dkv_copy.start()

    orders = ((0, 1, 2), (1, 2, 0), (2, 0, 1))
    sums = ((sum1_x, sum1_y, sum1_z), (sum2_x, sum2_y, sum2_z), (sum3_x, sum3_y, sum3_z))
    gots = ((got1_x, got1_y, got1_z), (got2_x, got2_y, got2_z), (got3_x, got3_y, got3_z))

    def ring_copy(stage, part, step):
        axis = orders[part][stage]
        return pltpu.make_async_remote_copy(
            src_ref=sums[stage][part].at[lax.rem(place[axis] + step, 4)],
            dst_ref=gots[stage][part].at[step - 1],
            send_sem=ring_send.at[stage, part, step - 1],
            recv_sem=ring_recv.at[stage, part, step - 1],
            device_id=along(axis, step), device_id_type=MESH)

    @pl.loop(0, pieces)
    def _(piece):
        hidden_copy(piece).wait_recv()

    dkv_copy.wait_recv()
    for step in (2, 1, 3, 0):
        x = lax.rem(place[0] + step, 4)
        for y_lo in range(2):
            groups = pl.ds(y_lo * 32 + x * 8, 8)
            own = hidden_t[groups, core].reshape(512, tok)
            paired = hidden_in[groups].reshape(512, tok)
            terms = (dot(own, dkv[0]) + dot(paired, dkv[1])).astype(BF16).reshape(4, 2, 64, 2 * head)
            for y_hi in range(2):
                y = y_hi * 2 + y_lo
                sum1_x[x, y] = terms[:, y_hi, 0:48, 0:head]
                sum1_y[y, :, x] = terms[:, y_hi, 0:48, head : 2 * head]
                sum1_z[:, x, y] = terms[:, y_hi, 48:64, :]
        if step > 0:
            ring_copy(0, 0, step).start()
    for part in (1, 2):
        for step in (2, 1, 3):
            ring_copy(0, part, step).start()

    for load in loads[6:]:
        load.wait()
    tile = 512

    @pl.loop(0, wide.shape[1] // tile)
    def _(index):
        rows = pl.ds(pl.multiple_of(index * tile, tile), tile)
        total = dot_rows(dq[...], qw[rows, :])
        total += dot_rows(dkv[0, :, 0:head], kw[rows, :])
        total += dot_rows(dkv[0, :, head : 2 * head], vw[rows, :])
        wide[:, rows] = total.astype(BF16)

    for stage in range(3):
        for part in range(3):
            for step in (1, 3, 2):
                ring_copy(stage, part, step).wait_recv()
            mine = place[orders[part][stage]]
            total = sums[stage][part][mine].astype(F32)
            for step in range(3):
                total += gots[stage][part][step].astype(F32)
            if stage < 2:
                sums[stage + 1][part][...] = total.astype(sums[stage + 1][part].dtype)
                for step in (2, 1, 3):
                    ring_copy(stage + 1, part, step).start()
            else:
                wgrad_ref[(slice(0, 48), slice(0, 48), slice(48, 64))[part],
                          (slice(0, head), slice(head, 2 * head), slice(0, 2 * head))[part]] = total

    @pl.loop(0, pieces)
    def _(piece):
        hidden_copy(piece).wait_send()

    dkv_copy.wait_send()
    for stage in range(3):
        for part in range(3):
            for step in (1, 2, 3):
                ring_copy(stage, part, step).wait_send()

    @pl.when(core == 0)
    def _():
        kv_copy(me, kv_send.at[chip], partner).wait_send()

    @pl.when(core == 1)
    def _():
        pair_copy(chip).wait_send()

    @pl.loop(chip + 1, chips)
    def _(target):
        kv_copy(me, kv_send.at[target], target * 2 + core).wait_send()

    @pl.loop(0, chip)
    def _(source):
        kv_copy(2 * source + core, kv_relay.at[source], partner).wait_send()
        pair_copy(source).wait_send()
        far_copy(source, chip).wait_send()


def finish_kernel(grad_ref, wgrad_ref, grad_out, wgrad_out, sem):
    copies = [
        pltpu.make_async_copy(grad_ref, grad_out, sem.at[0]),
        pltpu.make_async_copy(wgrad_ref, wgrad_out, sem.at[1]),
    ]
    for copy in copies:
        copy.start()
    for copy in copies:
        copy.wait()


def on_device(
    n_ctx, hidden, queries, key_rows, value_rows, out_grad, doc_ids, q_weight, k_weight, v_weight
):
    tok, head = key_rows.shape
    width = queries.shape[1]
    model = hidden.shape[1]
    heads = width // head
    chips = n_ctx // 2
    vmem = pl.BlockSpec(memory_space=pltpu.VMEM)
    hbm = pl.BlockSpec(memory_space=pl.ANY)
    dma = pltpu.SemaphoreType.DMA
    sums = []
    for lead in ((4, 4, 4), (4, 4), (4,)):
        for first in (lead, (3,) + lead[1:]):
            for block in ((48, head), (48, head), (16, 2 * head)):
                sums.append(pltpu.VMEM(first + block, BF16))
    grads = pl.pallas_call(
        functools.partial(backward_kernel, tok * n_ctx),
        out_shape=(pltpu.VMEM((tok, model), BF16), pltpu.VMEM((64, 2 * head), F32)),
        in_specs=[hbm] * 9,
        out_specs=(vmem, vmem),
        scratch_shapes=[
            pltpu.VMEM((tok, width), BF16),
            pltpu.VMEM((tok, head), BF16),
            pltpu.VMEM((tok, head), BF16),
            pltpu.VMEM((tok, width), BF16),
            pltpu.VMEM((1, tok), jnp.int32),
            pltpu.VMEM((n_ctx, tok + 16, 2 * head), BF16),
            pltpu.VMEM((head, heads * tok), BF16),
            pltpu.VMEM((head, heads * tok), BF16),
            pltpu.VMEM((n_ctx, tok, heads * tok), F32),
            pltpu.VMEM((n_ctx, 1, heads * tok), F32),
            pltpu.VMEM((1, heads * tok), F32),
            pltpu.VMEM((1, heads * tok), F32),
            pltpu.VMEM((tok, heads * tok), BF16),
            pltpu.VMEM((1, heads * tok), F32),
            pltpu.VMEM((head, heads * tok), F32),
            pltpu.VMEM((2, tok, 2 * head), F32),
            pltpu.VMEM((chips, tok, 2 * head), BF16),
            pltpu.VMEM((chips, tok, 2 * head), BF16),
            pltpu.VMEM((chips, tok, 2 * head), BF16),
            pltpu.VMEM((chips, tok, 2 * head), BF16),
            pltpu.VMEM((model // 128, 2, 64, tok), BF16),
            pltpu.VMEM((model // 128, 64, tok), BF16),
            pltpu.VMEM((model, width), BF16),
            pltpu.VMEM((model, head), BF16),
            pltpu.VMEM((model, head), BF16),
            pltpu.VMEM((tok, width), BF16),
            pltpu.VMEM((2, tok, 2 * head), BF16),
        ] + sums + [
            dma((chips,)), dma((chips,)), dma((n_ctx,)),
            dma((chips,)), dma((chips,)), dma((chips,)), dma((chips,)),
            dma((9,)), dma((17,)), dma((17,)), dma((3, 3, 3)), dma((3, 3, 3)),
        ],
        compiler_params=pltpu.CompilerParams(
            collective_id=0, has_side_effects=True, vmem_limit_bytes=56 * 1024 * 1024
        ),
    )(queries, key_rows, value_rows, out_grad, doc_ids.reshape(1, -1),
      hidden, q_weight, k_weight, v_weight)
    return pl.pallas_call(
        finish_kernel,
        out_shape=(
            jax.ShapeDtypeStruct((tok, model), BF16),
            jax.ShapeDtypeStruct((64, 2 * head), F32),
        ),
        in_specs=[vmem] * 2,
        out_specs=(hbm, hbm),
        scratch_shapes=[dma((2,))],
        compiler_params=pltpu.CompilerParams(vmem_limit_bytes=4 * 1024 * 1024),
    )(*grads)


def solution(mesh):
    tokens = P(("dp", "ctx"), None)
    return jax.shard_map(
        functools.partial(on_device, mesh.shape["ctx"]),
        mesh=mesh,
        in_specs=(tokens, tokens, tokens, tokens, tokens, P(("dp", "ctx")), P(), P(), P()),
        out_specs=(tokens, tokens),
        check_vma=False,
    )
```

```python
import functools

import jax
import jax.numpy as jnp
from jax import lax
from jax.experimental import pallas as pl
from jax.experimental.pallas import tpu as pltpu
from jax.sharding import PartitionSpec as P

MESH = pl.DeviceIdType.MESH
BF16 = jnp.bfloat16
F32 = jnp.float32
LOG2E = 1.4426950408889634
MASKED = -1e30


def dot(a, b):
    return jnp.dot(a, b, preferred_element_type=F32)


def dot_rows(a, b):
    return lax.dot_general(a, b, (((1,), (1,)), ((), ())), preferred_element_type=F32)


def backward_kernel(
    seq, q_hbm, k_hbm, v_hbm, do_hbm, docs_hbm, hidden_ref, qw_ref, kw_ref, vw_ref,
    wide, wgrad_ref,
    q_ref, k_ref, v_ref, do_ref, docs_ref, kv, q_t, do_t, probs, max_at, run_max, run_sum, score_grads, delta, dq_t, parts,
    pair_out, pair_in, far_out, far_in,
    hidden_t, hidden_in, qw, kw, vw, dq, dkv,
    sum1_x, sum1_y, sum1_z, got1_x, got1_y, got1_z,
    sum2_x, sum2_y, sum2_z, got2_x, got2_y, got2_z,
    sum3_x, sum3_y, sum3_z, got3_x, got3_y, got3_z,
    kv_send, kv_relay, kv_pass, kv_recv, pair_send, pair_recv, far_send, far_recv,
    load_sem, core_send, core_recv, ring_send, ring_recv,
):
    tok, head = k_ref.shape
    heads = q_ref.shape[1] // head
    chips = kv.shape[0] // 2
    scale = head ** -0.5
    row = lax.axis_index("dp")
    me = lax.axis_index("ctx")
    chip, core = me // 2, me % 2
    other = 1 - core
    partner = chip * 2 + other
    place = (row % 4, (chip % 2) * 2 + row // 4, chip // 2)

    def at(ctx):
        return (row, ctx)

    def along(axis, step):
        x, y, z = [lax.rem(p + step, 4) if i == axis else p for i, p in enumerate(place)]
        return ((y % 2) * 4 + x, z * 4 + (y // 2) * 2 + core)

    barrier = pltpu.get_barrier_semaphore()
    for step in range(1, chips):
        peer = lax.rem(chip + step, chips) * 2 + core
        pl.semaphore_signal(barrier, inc=1, device_id=at(peer), device_id_type=MESH)
    pl.semaphore_signal(barrier, inc=1, device_id=at(partner), device_id_type=MESH)
    for axis, step in ((0, 1), (0, 2), (0, 3), (1, 1), (1, 3)):
        pl.semaphore_signal(barrier, inc=1, device_id=along(axis, step), device_id_type=MESH)

    loads = [
        pltpu.make_async_copy(src, dst, load_sem.at[i])
        for i, (src, dst) in enumerate((
            (k_hbm, k_ref), (v_hbm, v_ref), (docs_hbm, docs_ref), (q_hbm, q_ref), (do_hbm, do_ref),
            (hidden_ref, wide), (qw_ref, qw), (kw_ref, kw), (vw_ref, vw)))
    ]
    for load in loads:
        load.start()
    for load in loads[:3]:
        load.wait()

    kv[me, 0:tok, 0:head] = k_ref[...]
    kv[me, 0:tok, head : 2 * head] = v_ref[...]
    last = docs_ref[...] - row * seq
    high, low = last // 64, last % 64
    digit = lax.broadcasted_iota(jnp.int32, (16, tok), 0)
    kv[me, tok : tok + 16, :] = jnp.where(digit == 0, high, low).astype(F32).astype(BF16)
    own_docs = last.astype(F32)

    def kv_copy(slot, send_sem, target):
        return pltpu.make_async_remote_copy(
            src_ref=kv.at[slot], dst_ref=kv.at[slot], send_sem=send_sem,
            recv_sem=kv_recv.at[slot], device_id=at(target), device_id_type=MESH)

    def pair_copy(index):
        return pltpu.make_async_remote_copy(
            src_ref=pair_out.at[index], dst_ref=pair_in.at[index], send_sem=pair_send.at[index],
            recv_sem=pair_recv.at[index], device_id=at(partner), device_id_type=MESH)

    def far_copy(index, slot):
        return pltpu.make_async_remote_copy(
            src_ref=far_out.at[index], dst_ref=far_in.at[slot], send_sem=far_send.at[index],
            recv_sem=far_recv.at[slot], device_id=at(index * 2 + core), device_id_type=MESH)

    for load in loads[3:5]:
        load.wait()
    for h in range(heads):
        cols = slice(h * head, (h + 1) * head)
        rows = slice(h * tok, (h + 1) * tok)
        q_t[:, rows] = q_ref[:, cols].T
        do_t[:, rows] = do_ref[:, cols].T
    pl.semaphore_wait(barrier, chips + 5)

    plane, side = chip // 2, chip % 2
    neighbour = (2 * plane + 1 - side) * 2 + core
    passes_on = plane >= 2
    passed_chip = (3 - plane) * 2 + side

    def sent_straight(target):
        return (target // 2 + plane != 3) | (target % 2 == side)

    def source_of(back):
        k = back - side
        far_plane = jnp.where((k == 1) | (k == 4), 0, jnp.where(k <= 3, 2, 1))
        far_side = jnp.where((k == 1) | (k == 2) | (k == 5), side, 1 - side)
        near_plane = jnp.where(k <= 2, 1, 0)
        near_side = jnp.where(k % 2 == 1, side, 1 - side)
        return jnp.where(
            (k >= 1) & (plane == 3), 2 * far_plane + far_side,
            jnp.where((k >= 1) & (plane == 2), 2 * near_plane + near_side, chip - back))

    @pl.when(core == 0)
    def _():
        kv_copy(me, kv_send.at[chip], partner).start()

    @pl.loop(0, chips - 1 - chip)
    def _(i):
        target = chips - 1 - i

        @pl.when(sent_straight(target) & (target // 2 != plane + 2))
        def _():
            kv_copy(me, kv_send.at[target], target * 2 + core).start()

    run_max[...] = jnp.full_like(run_max, MASKED)
    run_sum[...] = jnp.zeros_like(run_sum)
    delta[...] = jnp.zeros_like(delta)
    dq_t[...] = jnp.zeros_like(dq_t)

    pieces = 16
    piece_groups = hidden_t.shape[0] // pieces

    def hidden_copy(piece):
        groups = pl.ds(piece * piece_groups, piece_groups)
        return pltpu.make_async_remote_copy(
            src_ref=hidden_t.at[groups, other], dst_ref=hidden_in.at[groups],
            send_sem=core_send.at[piece], recv_sem=core_recv.at[piece],
            device_id=at(partner), device_id_type=MESH)

    @pl.loop(0, 2 * (chip + 1))
    def _(i):
        last_step = i == 2 * chip + 1
        second = jnp.where(last_step | ((i > 0) & (i % 2 == 0)), 1, 0)
        back = jnp.where(last_step, chip, jnp.where(second == 1, i // 2 - 1, (i + 1) // 2))
        source = source_of(back)
        slot = 2 * source + jnp.where(second == 0, core, other)
        skipped = (back == 0) & (second == 1) & (core == 0)

        @pl.when((i > 0) & jnp.logical_not(skipped))
        def _():
            kv_copy(slot, kv_relay.at[source], partner).wait_recv()

        @pl.when((i > 0) & (second == 0))
        def _():
            kv_copy(slot, kv_relay.at[source], partner).start()

        @pl.when((second == 0) & passes_on & (source == passed_chip))
        def _():
            kv_copy(slot, kv_pass.at[0], neighbour).start()

        @pl.when(jnp.logical_not(skipped))
        def _():
            keys = kv[slot, 0:tok, 0:head]
            values = kv[slot, 0:tok, head : 2 * head]
            digits = kv[slot, tok : tok + 16, :].astype(F32)
            key_docs = digits[0:1, :] * 64.0 + digits[1:2, :]
            key_docs = jnp.broadcast_to(key_docs, (tok, tok)).T
            key_pos = lax.broadcasted_iota(jnp.int32, (tok, tok), 0)
            query_pos = lax.broadcasted_iota(jnp.int32, (tok, tok), 1)
            allowed = (key_docs == own_docs) & (key_pos - query_pos <= (me - slot) * tok)
            for h in range(heads):
                rows = slice(h * tok, (h + 1) * tok)
                scores = dot(keys, q_t[:, rows]) * (scale * LOG2E)
                scores = jnp.where(allowed, scores, MASKED)
                old_max = run_max[:, rows]
                new_max = jnp.maximum(old_max, jnp.max(scores, axis=0, keepdims=True))
                weights = jnp.exp2(scores - new_max)
                shrink = jnp.exp2(old_max - new_max)
                run_max[:, rows] = new_max
                max_at[slot, :, rows] = new_max
                run_sum[:, rows] = run_sum[:, rows] * shrink + jnp.sum(weights, axis=0, keepdims=True)
                probs[slot, :, rows] = weights
                prob_grad = dot(values, do_t[:, rows])
                delta[:, rows] = delta[:, rows] * shrink + jnp.sum(
                    weights * prob_grad, axis=0, keepdims=True)

        @pl.when(i == 0)
        def _():
            loads[5].wait()

            @pl.loop(0, hidden_t.shape[0])
            def _(group):
                turned = wide[:, pl.ds(pl.multiple_of(group * 128, 128), 128)].T
                hidden_t[group, 0] = turned[0:64]
                hidden_t[group, 1] = turned[64:128]

            @pl.when(plane < 2)
            def _():
                kv_copy(me, kv_send.at[passed_chip], passed_chip * 2 + core).wait_send()
                for target_side in range(2):
                    target = 2 * (plane + 2) + target_side
                    kv_copy(me, kv_send.at[target], target * 2 + core).start()

    run_sum[...] = 1.0 / run_sum[...]
    delta[...] = delta[...] * run_sum[...]

    def target_of(turn):
        across = (chip + 1) // 2
        own_side = chip % 2
        return jnp.where(turn == chip, chip, jnp.where(
            turn < across, 2 * turn + 1 - own_side, 2 * (turn - across) + own_side))

    @pl.loop(0, 2 * (chip + 1))
    def _(i):
        turn, second = i // 2, i % 2
        source = target_of(turn)
        slot = 2 * source + jnp.where(second == 0, other, core)
        own_chip = source == chip
        skipped = own_chip & (second == 0) & (core == 0)

        @pl.when(jnp.logical_not(skipped))
        def _():
            keys_t = kv[slot, 0:tok, 0:head].T
            values = kv[slot, 0:tok, head : 2 * head]
            key_part = jnp.zeros((tok, head), F32)
            value_part = jnp.zeros((tok, head), F32)
            for h in range(heads):
                cols = slice(h * head, (h + 1) * head)
                rows = slice(h * tok, (h + 1) * tok)
                factor = jnp.exp2(max_at[slot, :, rows] - run_max[:, rows]) * run_sum[:, rows]
                prob = probs[slot, :, rows] * factor
                prob_grad = dot(values, do_t[:, rows])
                score_grad = (scale * prob * (prob_grad - delta[:, rows])).astype(BF16)
                value_part += dot(prob.astype(BF16), do_ref[:, cols])
                key_part += dot(score_grad, q_ref[:, cols])
                score_grads[:, rows] = score_grad
            dq_t[...] += dot(keys_t, score_grads[...])
            parts[second, :, 0:head] = key_part
            parts[second, :, head : 2 * head] = value_part

        @pl.when((second == 0) & jnp.logical_not(skipped))
        def _():
            pair_out[source] = parts[0].astype(BF16)
            pair_copy(source).start()

        @pl.when((second == 0) & (turn > 0))
        def _():
            before = target_of(turn - 1)
            pair_copy(before).wait_recv()
            far_out[before] = (parts[1] + pair_in[before].astype(F32)).astype(BF16)
            far_copy(before, chip).start()

        hidden_copy(i).start()

    @pl.loop(2 * (chip + 1), pieces)
    def _(piece):
        hidden_copy(piece).start()

    for h in range(heads):
        cols = slice(h * head, (h + 1) * head)
        rows = slice(h * tok, (h + 1) * tok)
        dq[:, cols] = dq_t[:, rows].T.astype(BF16)

    @pl.when(core == 0)
    def _():
        pair_copy(chip).wait_recv()
        parts[1] += pair_in[chip].astype(F32)

    @pl.loop(chip + 1, chips)
    def _(source):
        far_copy(source, source).wait_recv()
        parts[1] += far_in[source].astype(F32)

    dkv[0] = parts[1].astype(BF16)
    dkv_copy = pltpu.make_async_remote_copy(
        src_ref=dkv.at[0], dst_ref=dkv.at[1], send_sem=core_send.at[pieces],
        recv_sem=core_recv.at[pieces], device_id=at(partner), device_id_type=MESH)
    dkv_copy.start()

    orders = ((0, 1, 2), (1, 2, 0), (2, 0, 1))
    sums = ((sum1_x, sum1_y, sum1_z), (sum2_x, sum2_y, sum2_z), (sum3_x, sum3_y, sum3_z))
    gots = ((got1_x, got1_y, got1_z), (got2_x, got2_y, got2_z), (got3_x, got3_y, got3_z))

    def ring_copy(stage, part, step):
        axis = orders[part][stage]
        return pltpu.make_async_remote_copy(
            src_ref=sums[stage][part].at[lax.rem(place[axis] + step, 4)],
            dst_ref=gots[stage][part].at[step - 1],
            send_sem=ring_send.at[stage, part, step - 1],
            recv_sem=ring_recv.at[stage, part, step - 1],
            device_id=along(axis, step), device_id_type=MESH)

    def quarter_copy(part, step, x):
        axis = orders[part][0]
        return pltpu.make_async_remote_copy(
            src_ref=sums[0][part].at[lax.rem(place[axis] + step, 4), x],
            dst_ref=gots[0][part].at[step - 1, x],
            send_sem=ring_send.at[0, part, step - 1],
            recv_sem=ring_recv.at[0, part, step - 1],
            device_id=along(axis, step), device_id_type=MESH)

    @pl.loop(0, pieces)
    def _(piece):
        hidden_copy(piece).wait_recv()

    dkv_copy.wait_recv()
    for step in (2, 1, 3, 0):
        x = lax.rem(place[0] + step, 4)
        for y_lo in range(2):
            groups = pl.ds(y_lo * 32 + x * 8, 8)
            own = hidden_t[groups, core].reshape(512, tok)
            paired = hidden_in[groups].reshape(512, tok)
            terms = (dot(own, dkv[0]) + dot(paired, dkv[1])).astype(BF16).reshape(4, 2, 64, 2 * head)
            for y_hi in range(2):
                y = y_hi * 2 + y_lo
                sum1_x[x, y] = terms[:, y_hi, 0:48, 0:head]
                sum1_y[y, x] = terms[:, y_hi, 0:48, head : 2 * head]
                sum1_z[:, x, y] = terms[:, y_hi, 48:64, :]
        if step > 0:
            ring_copy(0, 0, step).start()
        for part in (1, 2):
            for away in (2, 1, 3):
                quarter_copy(part, away, x).start()

    for load in loads[6:]:
        load.wait()
    tile = 512

    @pl.loop(0, wide.shape[1] // tile)
    def _(index):
        rows = pl.ds(pl.multiple_of(index * tile, tile), tile)
        total = dot_rows(dq[...], qw[rows, :])
        total += dot_rows(dkv[0, :, 0:head], kw[rows, :])
        total += dot_rows(dkv[0, :, head : 2 * head], vw[rows, :])
        wide[:, rows] = total.astype(BF16)

    for stage in range(3):
        for part in range(3):
            for step in (1, 3, 2):
                ring_copy(stage, part, step).wait_recv()
            mine = place[orders[part][stage]]
            if stage == 2:
                total = sums[2][part][mine].astype(F32)
                for came in range(3):
                    total += gots[2][part][came].astype(F32)
                wgrad_ref[(slice(0, 48), slice(0, 48), slice(48, 64))[part],
                          (slice(0, head), slice(head, 2 * head), slice(0, 2 * head))[part]] = total
                continue
            for step in (2, 1, 3, 0):
                index = lax.rem(place[orders[part][stage + 1]] + step, 4)
                where = (slice(None), index) if (stage, part) == (0, 1) else (index,)
                total = sums[stage][part][(mine,) + where].astype(F32)
                for came in range(3):
                    total += gots[stage][part][(came,) + where].astype(F32)
                sums[stage + 1][part][index] = total.astype(BF16)
                if step > 0:
                    ring_copy(stage + 1, part, step).start()

    @pl.loop(0, pieces)
    def _(piece):
        hidden_copy(piece).wait_send()

    dkv_copy.wait_send()
    for stage in range(3):
        for part in range(3):
            for step in (1, 2, 3):
                ring_copy(stage, part, step).wait_send()

    @pl.when(core == 0)
    def _():
        kv_copy(me, kv_send.at[chip], partner).wait_send()

    @pl.when(core == 1)
    def _():
        pair_copy(chip).wait_send()

    @pl.loop(chip + 1, chips)
    def _(target):
        @pl.when(sent_straight(target) & ((plane >= 2) | (target != passed_chip)))
        def _():
            kv_copy(me, kv_send.at[target], target * 2 + core).wait_send()

    @pl.when(passes_on)
    def _():
        kv_copy(2 * passed_chip + core, kv_pass.at[0], neighbour).wait_send()

    @pl.loop(0, chip)
    def _(source):
        kv_copy(2 * source + core, kv_relay.at[source], partner).wait_send()
        pair_copy(source).wait_send()
        far_copy(source, chip).wait_send()


def finish_kernel(grad_ref, wgrad_ref, grad_out, wgrad_out, sem):
    copies = [
        pltpu.make_async_copy(grad_ref, grad_out, sem.at[0]),
        pltpu.make_async_copy(wgrad_ref, wgrad_out, sem.at[1]),
    ]
    for copy in copies:
        copy.start()
    for copy in copies:
        copy.wait()


def on_device(
    n_ctx, hidden, queries, key_rows, value_rows, out_grad, doc_ids, q_weight, k_weight, v_weight
):
    tok, head = key_rows.shape
    width = queries.shape[1]
    model = hidden.shape[1]
    heads = width // head
    chips = n_ctx // 2
    vmem = pl.BlockSpec(memory_space=pltpu.VMEM)
    hbm = pl.BlockSpec(memory_space=pl.ANY)
    dma = pltpu.SemaphoreType.DMA
    sums = []
    for lead in ((4, 4, 4), (4, 4), (4,)):
        for first in (lead, (3,) + lead[1:]):
            for block in ((48, head), (48, head), (16, 2 * head)):
                sums.append(pltpu.VMEM(first + block, BF16))
    grads = pl.pallas_call(
        functools.partial(backward_kernel, tok * n_ctx),
        out_shape=(pltpu.VMEM((tok, model), BF16), pltpu.VMEM((64, 2 * head), F32)),
        in_specs=[hbm] * 9,
        out_specs=(vmem, vmem),
        scratch_shapes=[
            pltpu.VMEM((tok, width), BF16),
            pltpu.VMEM((tok, head), BF16),
            pltpu.VMEM((tok, head), BF16),
            pltpu.VMEM((tok, width), BF16),
            pltpu.VMEM((1, tok), jnp.int32),
            pltpu.VMEM((n_ctx, tok + 16, 2 * head), BF16),
            pltpu.VMEM((head, heads * tok), BF16),
            pltpu.VMEM((head, heads * tok), BF16),
            pltpu.VMEM((n_ctx, tok, heads * tok), F32),
            pltpu.VMEM((n_ctx, 1, heads * tok), F32),
            pltpu.VMEM((1, heads * tok), F32),
            pltpu.VMEM((1, heads * tok), F32),
            pltpu.VMEM((tok, heads * tok), BF16),
            pltpu.VMEM((1, heads * tok), F32),
            pltpu.VMEM((head, heads * tok), F32),
            pltpu.VMEM((2, tok, 2 * head), F32),
            pltpu.VMEM((chips, tok, 2 * head), BF16),
            pltpu.VMEM((chips, tok, 2 * head), BF16),
            pltpu.VMEM((chips, tok, 2 * head), BF16),
            pltpu.VMEM((chips, tok, 2 * head), BF16),
            pltpu.VMEM((model // 128, 2, 64, tok), BF16),
            pltpu.VMEM((model // 128, 64, tok), BF16),
            pltpu.VMEM((model, width), BF16),
            pltpu.VMEM((model, head), BF16),
            pltpu.VMEM((model, head), BF16),
            pltpu.VMEM((tok, width), BF16),
            pltpu.VMEM((2, tok, 2 * head), BF16),
        ] + sums + [
            dma((chips,)), dma((chips,)), dma((1,)), dma((n_ctx,)),
            dma((chips,)), dma((chips,)), dma((chips,)), dma((chips,)),
            dma((9,)), dma((17,)), dma((17,)), dma((3, 3, 3)), dma((3, 3, 3)),
        ],
        compiler_params=pltpu.CompilerParams(
            collective_id=0, has_side_effects=True, vmem_limit_bytes=56 * 1024 * 1024
        ),
    )(queries, key_rows, value_rows, out_grad, doc_ids.reshape(1, -1),
      hidden, q_weight, k_weight, v_weight)
    return pl.pallas_call(
        finish_kernel,
        out_shape=(
            jax.ShapeDtypeStruct((tok, model), BF16),
            jax.ShapeDtypeStruct((64, 2 * head), F32),
        ),
        in_specs=[vmem] * 2,
        out_specs=(hbm, hbm),
        scratch_shapes=[dma((2,))],
        compiler_params=pltpu.CompilerParams(vmem_limit_bytes=4 * 1024 * 1024),
    )(*grads)


def solution(mesh):
    tokens = P(("dp", "ctx"), None)
    return jax.shard_map(
        functools.partial(on_device, mesh.shape["ctx"]),
        mesh=mesh,
        in_specs=(tokens, tokens, tokens, tokens, tokens, P(("dp", "ctx")), P(), P(), P()),
        out_specs=(tokens, tokens),
        check_vma=False,
    )
```

```python
import functools

import jax
import jax.numpy as jnp
from jax import lax
from jax.experimental import pallas as pl
from jax.experimental.pallas import tpu as pltpu
from jax.sharding import PartitionSpec as P

MESH = pl.DeviceIdType.MESH
BF16 = jnp.bfloat16
F32 = jnp.float32
LOG2E = 1.4426950408889634
MASKED = -1e30


def dot(a, b):
    return jnp.dot(a, b, preferred_element_type=F32)


def dot_rows(a, b):
    return lax.dot_general(a, b, (((1,), (1,)), ((), ())), preferred_element_type=F32)


def backward_kernel(
    seq, q_hbm, k_hbm, v_hbm, do_hbm, docs_hbm, hidden_ref, qw_ref, kw_ref, vw_ref,
    wide, wgrad_ref,
    q_ref, k_ref, v_ref, do_ref, docs_ref, kv, q_t, do_t, probs, max_at, run_max, run_sum, score_grads, delta, dq_t, parts,
    pair_out, pair_in, far_out, far_in, joined,
    hidden_t, hidden_in, qw, kw, vw, dq, dkv,
    sum1_x, sum1_y, sum1_z, got1_x, got1_y, got1_z,
    sum2_x, sum2_y, sum2_z, got2_x, got2_y, got2_z,
    sum3_x, sum3_y, sum3_z, got3_x, got3_y, got3_z,
    kv_send, kv_relay, kv_pass, kv_recv, pair_send, pair_recv, far_send, far_recv, join_sem,
    load_sem, core_send, core_recv, ring_send, ring_recv,
):
    tok, head = k_ref.shape
    heads = q_ref.shape[1] // head
    chips = kv.shape[0] // 2
    scale = head ** -0.5
    row = lax.axis_index("dp")
    me = lax.axis_index("ctx")
    chip, core = me // 2, me % 2
    other = 1 - core
    partner = chip * 2 + other
    place = (row % 4, (chip % 2) * 2 + row // 4, chip // 2)

    def at(ctx):
        return (row, ctx)

    def along(axis, step):
        x, y, z = [lax.rem(p + step, 4) if i == axis else p for i, p in enumerate(place)]
        return ((y % 2) * 4 + x, z * 4 + (y // 2) * 2 + core)

    barrier = pltpu.get_barrier_semaphore()
    for step in range(1, chips):
        peer = lax.rem(chip + step, chips) * 2 + core
        pl.semaphore_signal(barrier, inc=1, device_id=at(peer), device_id_type=MESH)
    pl.semaphore_signal(barrier, inc=1, device_id=at(partner), device_id_type=MESH)
    for axis, step in ((0, 1), (0, 2), (0, 3), (1, 1), (1, 3)):
        pl.semaphore_signal(barrier, inc=1, device_id=along(axis, step), device_id_type=MESH)

    loads = [
        pltpu.make_async_copy(src, dst, load_sem.at[i])
        for i, (src, dst) in enumerate((
            (k_hbm, k_ref), (v_hbm, v_ref), (docs_hbm, docs_ref), (q_hbm, q_ref), (do_hbm, do_ref),
            (hidden_ref, wide), (qw_ref, qw), (kw_ref, kw), (vw_ref, vw)))
    ]
    for load in loads:
        load.start()
    for load in loads[:3]:
        load.wait()

    kv[me, 0:tok, 0:head] = k_ref[...]
    kv[me, 0:tok, head : 2 * head] = v_ref[...]
    last = docs_ref[...] - row * seq
    high, low = last // 64, last % 64
    digit = lax.broadcasted_iota(jnp.int32, (16, tok), 0)
    kv[me, tok : tok + 16, :] = jnp.where(digit == 0, high, low).astype(F32).astype(BF16)
    own_docs = last.astype(F32)

    def kv_copy(slot, send_sem, target):
        return pltpu.make_async_remote_copy(
            src_ref=kv.at[slot], dst_ref=kv.at[slot], send_sem=send_sem,
            recv_sem=kv_recv.at[slot], device_id=at(target), device_id_type=MESH)

    def pair_copy(index):
        return pltpu.make_async_remote_copy(
            src_ref=pair_out.at[index], dst_ref=pair_in.at[index], send_sem=pair_send.at[index],
            recv_sem=pair_recv.at[index], device_id=at(partner), device_id_type=MESH)

    def far_copy(index, slot):
        return pltpu.make_async_remote_copy(
            src_ref=far_out.at[index], dst_ref=far_in.at[slot], send_sem=far_send.at[index],
            recv_sem=far_recv.at[slot], device_id=at(index * 2 + core), device_id_type=MESH)

    for load in loads[3:5]:
        load.wait()
    for h in range(heads):
        cols = slice(h * head, (h + 1) * head)
        rows = slice(h * tok, (h + 1) * tok)
        q_t[:, rows] = q_ref[:, cols].T
        do_t[:, rows] = do_ref[:, cols].T
    pl.semaphore_wait(barrier, chips + 5)

    plane, side = chip // 2, chip % 2
    neighbour = (2 * plane + 1 - side) * 2 + core
    passes_on = plane >= 2
    passed_chip = (3 - plane) * 2 + side

    def sent_straight(target):
        return (target // 2 + plane != 3) | (target % 2 == side)

    def source_of(back):
        k = back - side
        far_plane = jnp.where((k == 1) | (k == 4), 0, jnp.where(k <= 3, 2, 1))
        far_side = jnp.where((k == 1) | (k == 2) | (k == 5), side, 1 - side)
        near_plane = jnp.where(k <= 2, 1, 0)
        near_side = jnp.where(k % 2 == 1, side, 1 - side)
        return jnp.where(
            (k >= 1) & (plane == 3), 2 * far_plane + far_side,
            jnp.where((k >= 1) & (plane == 2), 2 * near_plane + near_side, chip - back))

    @pl.when(core == 0)
    def _():
        kv_copy(me, kv_send.at[chip], partner).start()

    @pl.loop(0, chips - 1 - chip)
    def _(i):
        target = chips - 1 - i

        @pl.when(sent_straight(target) & (target // 2 != plane + 2))
        def _():
            kv_copy(me, kv_send.at[target], target * 2 + core).start()

    run_max[...] = jnp.full_like(run_max, MASKED)
    run_sum[...] = jnp.zeros_like(run_sum)
    delta[...] = jnp.zeros_like(delta)
    dq_t[...] = jnp.zeros_like(dq_t)

    pieces = 16
    piece_groups = hidden_t.shape[0] // pieces

    def hidden_copy(piece):
        groups = pl.ds(piece * piece_groups, piece_groups)
        return pltpu.make_async_remote_copy(
            src_ref=hidden_t.at[groups, other], dst_ref=hidden_in.at[groups],
            send_sem=core_send.at[piece], recv_sem=core_recv.at[piece],
            device_id=at(partner), device_id_type=MESH)

    @pl.loop(0, 2 * (chip + 1))
    def _(i):
        last_step = i == 2 * chip + 1
        second = jnp.where(last_step | ((i > 0) & (i % 2 == 0)), 1, 0)
        back = jnp.where(last_step, chip, jnp.where(second == 1, i // 2 - 1, (i + 1) // 2))
        source = source_of(back)
        slot = 2 * source + jnp.where(second == 0, core, other)
        skipped = (back == 0) & (second == 1) & (core == 0)

        @pl.when((i > 0) & jnp.logical_not(skipped))
        def _():
            kv_copy(slot, kv_relay.at[source], partner).wait_recv()

        @pl.when((i > 0) & (second == 0))
        def _():
            kv_copy(slot, kv_relay.at[source], partner).start()

        @pl.when((second == 0) & passes_on & (source == passed_chip))
        def _():
            kv_copy(slot, kv_pass.at[0], neighbour).start()

        @pl.when(jnp.logical_not(skipped))
        def _():
            keys = kv[slot, 0:tok, 0:head]
            values = kv[slot, 0:tok, head : 2 * head]
            digits = kv[slot, tok : tok + 16, :].astype(F32)
            key_docs = digits[0:1, :] * 64.0 + digits[1:2, :]
            key_docs = jnp.broadcast_to(key_docs, (tok, tok)).T
            key_pos = lax.broadcasted_iota(jnp.int32, (tok, tok), 0)
            query_pos = lax.broadcasted_iota(jnp.int32, (tok, tok), 1)
            allowed = (key_docs == own_docs) & (key_pos - query_pos <= (me - slot) * tok)
            for h in range(heads):
                rows = slice(h * tok, (h + 1) * tok)
                scores = dot(keys, q_t[:, rows]) * (scale * LOG2E)
                scores = jnp.where(allowed, scores, MASKED)
                old_max = run_max[:, rows]
                new_max = jnp.maximum(old_max, jnp.max(scores, axis=0, keepdims=True))
                weights = jnp.exp2(scores - new_max)
                shrink = jnp.exp2(old_max - new_max)
                run_max[:, rows] = new_max
                max_at[slot, :, rows] = new_max
                run_sum[:, rows] = run_sum[:, rows] * shrink + jnp.sum(weights, axis=0, keepdims=True)
                probs[slot, :, rows] = weights
                prob_grad = dot(values, do_t[:, rows])
                delta[:, rows] = delta[:, rows] * shrink + jnp.sum(
                    weights * prob_grad, axis=0, keepdims=True)

        @pl.when(i == 0)
        def _():
            loads[5].wait()

            @pl.loop(0, hidden_t.shape[0])
            def _(group):
                turned = wide[:, pl.ds(pl.multiple_of(group * 128, 128), 128)].T
                hidden_t[group, 0] = turned[0:64]
                hidden_t[group, 1] = turned[64:128]

            @pl.when(plane < 2)
            def _():
                kv_copy(me, kv_send.at[passed_chip], passed_chip * 2 + core).wait_send()
                for target_side in range(2):
                    target = 2 * (plane + 2) + target_side
                    kv_copy(me, kv_send.at[target], target * 2 + core).start()

    run_sum[...] = 1.0 / run_sum[...]
    delta[...] = delta[...] * run_sum[...]

    def target_of(turn):
        across = (chip + 1) // 2
        own_side = chip % 2
        return jnp.where(turn == chip, chip, jnp.where(
            turn < across, 2 * turn + 1 - own_side, 2 * (chip - 1 - turn) + own_side))

    def join_copy():
        return pltpu.make_async_remote_copy(
            src_ref=far_out.at[1 - side], dst_ref=joined, send_sem=join_sem.at[0],
            recv_sem=join_sem.at[1], device_id=at(neighbour), device_id_type=MESH)

    @pl.loop(0, 2 * (chip + 1))
    def _(i):
        turn, second = i // 2, i % 2
        source = target_of(turn)
        slot = 2 * source + jnp.where(second == 0, other, core)
        own_chip = source == chip
        skipped = own_chip & (second == 0) & (core == 0)

        @pl.when(jnp.logical_not(skipped))
        def _():
            keys_t = kv[slot, 0:tok, 0:head].T
            values = kv[slot, 0:tok, head : 2 * head]
            key_part = jnp.zeros((tok, head), F32)
            value_part = jnp.zeros((tok, head), F32)
            for h in range(heads):
                cols = slice(h * head, (h + 1) * head)
                rows = slice(h * tok, (h + 1) * tok)
                factor = jnp.exp2(max_at[slot, :, rows] - run_max[:, rows]) * run_sum[:, rows]
                prob = probs[slot, :, rows] * factor
                prob_grad = dot(values, do_t[:, rows])
                score_grad = (scale * prob * (prob_grad - delta[:, rows])).astype(BF16)
                value_part += dot(prob.astype(BF16), do_ref[:, cols])
                key_part += dot(score_grad, q_ref[:, cols])
                score_grads[:, rows] = score_grad
            dq_t[...] += dot(keys_t, score_grads[...])
            parts[second, :, 0:head] = key_part
            parts[second, :, head : 2 * head] = value_part

        @pl.when((second == 0) & jnp.logical_not(skipped))
        def _():
            pair_out[source] = parts[0].astype(BF16)
            pair_copy(source).start()

        @pl.when((second == 0) & (turn > 0))
        def _():
            before = target_of(turn - 1)
            pair_copy(before).wait_recv()

            @pl.when((plane >= 2) & (before == side))
            def _():
                join_copy().wait_recv()
                parts[1] += joined[...].astype(F32)

            far_out[before] = (parts[1] + pair_in[before].astype(F32)).astype(BF16)

            @pl.when((plane >= 2) & (before == 1 - side))
            def _():
                join_copy().start()

            @pl.when((plane < 2) | (before != 1 - side))
            def _():
                far_copy(before, chip).start()

        hidden_copy(i).start()

    @pl.loop(2 * (chip + 1), pieces)
    def _(piece):
        hidden_copy(piece).start()

    for h in range(heads):
        cols = slice(h * head, (h + 1) * head)
        rows = slice(h * tok, (h + 1) * tok)
        dq[:, cols] = dq_t[:, rows].T.astype(BF16)

    @pl.when(core == 0)
    def _():
        pair_copy(chip).wait_recv()
        parts[1] += pair_in[chip].astype(F32)

    @pl.loop(chip + 1, chips)
    def _(source):
        @pl.when((plane > 0) | (source < 4) | (source % 2 == side))
        def _():
            far_copy(source, source).wait_recv()
            parts[1] += far_in[source].astype(F32)

    dkv[0] = parts[1].astype(BF16)
    dkv_copy = pltpu.make_async_remote_copy(
        src_ref=dkv.at[0], dst_ref=dkv.at[1], send_sem=core_send.at[pieces],
        recv_sem=core_recv.at[pieces], device_id=at(partner), device_id_type=MESH)
    dkv_copy.start()

    orders = ((0, 1, 2), (1, 2, 0), (2, 0, 1))
    sums = ((sum1_x, sum1_y, sum1_z), (sum2_x, sum2_y, sum2_z), (sum3_x, sum3_y, sum3_z))
    gots = ((got1_x, got1_y, got1_z), (got2_x, got2_y, got2_z), (got3_x, got3_y, got3_z))

    def ring_copy(stage, part, step):
        axis = orders[part][stage]
        return pltpu.make_async_remote_copy(
            src_ref=sums[stage][part].at[lax.rem(place[axis] + step, 4)],
            dst_ref=gots[stage][part].at[step - 1],
            send_sem=ring_send.at[stage, part, step - 1],
            recv_sem=ring_recv.at[stage, part, step - 1],
            device_id=along(axis, step), device_id_type=MESH)

    def quarter_copy(part, step, x):
        axis = orders[part][0]
        return pltpu.make_async_remote_copy(
            src_ref=sums[0][part].at[lax.rem(place[axis] + step, 4), x],
            dst_ref=gots[0][part].at[step - 1, x],
            send_sem=ring_send.at[0, part, step - 1],
            recv_sem=ring_recv.at[0, part, step - 1],
            device_id=along(axis, step), device_id_type=MESH)

    @pl.loop(0, pieces)
    def _(piece):
        hidden_copy(piece).wait_recv()

    for step in range(4):
        x = lax.rem(place[0] + step, 4)
        for y_lo in range(2):
            own = hidden_t[pl.ds(y_lo * 32 + x * 8, 8), core].reshape(512, tok)
            own_terms = dot(own, dkv[0])
            probs[2 * step + y_lo, :, 0 : 2 * head] = own_terms[0:256]
            probs[2 * step + y_lo, :, 2 * head : 4 * head] = own_terms[256:512]
    dkv_copy.wait_recv()
    for step in (2, 1, 3, 0):
        x = lax.rem(place[0] + step, 4)
        for y_lo in range(2):
            paired = hidden_in[pl.ds(y_lo * 32 + x * 8, 8)].reshape(512, tok)
            own_terms = jnp.concatenate(
                [probs[2 * step + y_lo, :, 0 : 2 * head],
                 probs[2 * step + y_lo, :, 2 * head : 4 * head]], axis=0)
            terms = (own_terms + dot(paired, dkv[1])).astype(BF16).reshape(4, 2, 64, 2 * head)
            for y_hi in range(2):
                y = y_hi * 2 + y_lo
                sum1_x[x, y] = terms[:, y_hi, 0:48, 0:head]
                sum1_y[y, x] = terms[:, y_hi, 0:48, head : 2 * head]
                sum1_z[:, x, y] = terms[:, y_hi, 48:64, :]
        if step > 0:
            ring_copy(0, 0, step).start()
        for part in (1, 2):
            for away in (2, 1, 3):
                quarter_copy(part, away, x).start()

    for load in loads[6:]:
        load.wait()
    tile = 512

    @pl.loop(0, wide.shape[1] // tile)
    def _(index):
        rows = pl.ds(pl.multiple_of(index * tile, tile), tile)
        total = dot_rows(dq[...], qw[rows, :])
        total += dot_rows(dkv[0, :, 0:head], kw[rows, :])
        total += dot_rows(dkv[0, :, head : 2 * head], vw[rows, :])
        wide[:, rows] = total.astype(BF16)

    for stage in range(3):
        for part in range(3):
            for step in (1, 3, 2):
                ring_copy(stage, part, step).wait_recv()
            mine = place[orders[part][stage]]
            if stage == 2:
                total = sums[2][part][mine].astype(F32)
                for came in range(3):
                    total += gots[2][part][came].astype(F32)
                wgrad_ref[(slice(0, 48), slice(0, 48), slice(48, 64))[part],
                          (slice(0, head), slice(head, 2 * head), slice(0, 2 * head))[part]] = total
                continue
            for step in (2, 1, 3, 0):
                index = lax.rem(place[orders[part][stage + 1]] + step, 4)
                where = (slice(None), index) if (stage, part) == (0, 1) else (index,)
                total = sums[stage][part][(mine,) + where].astype(F32)
                for came in range(3):
                    total += gots[stage][part][(came,) + where].astype(F32)
                sums[stage + 1][part][index] = total.astype(BF16)
                if step > 0:
                    ring_copy(stage + 1, part, step).start()

    @pl.loop(0, pieces)
    def _(piece):
        hidden_copy(piece).wait_send()

    dkv_copy.wait_send()
    for stage in range(3):
        for part in range(3):
            for step in (1, 2, 3):
                ring_copy(stage, part, step).wait_send()

    @pl.when(core == 0)
    def _():
        kv_copy(me, kv_send.at[chip], partner).wait_send()

    @pl.when(core == 1)
    def _():
        pair_copy(chip).wait_send()

    @pl.loop(chip + 1, chips)
    def _(target):
        @pl.when(sent_straight(target) & ((plane >= 2) | (target != passed_chip)))
        def _():
            kv_copy(me, kv_send.at[target], target * 2 + core).wait_send()

    @pl.when(passes_on)
    def _():
        kv_copy(2 * passed_chip + core, kv_pass.at[0], neighbour).wait_send()

    @pl.loop(0, chip)
    def _(source):
        kv_copy(2 * source + core, kv_relay.at[source], partner).wait_send()
        pair_copy(source).wait_send()

        @pl.when((plane < 2) | (source != 1 - side))
        def _():
            far_copy(source, chip).wait_send()

    @pl.when(plane >= 2)
    def _():
        join_copy().wait_send()


def finish_kernel(grad_ref, wgrad_ref, grad_out, wgrad_out, sem):
    copies = [
        pltpu.make_async_copy(grad_ref, grad_out, sem.at[0]),
        pltpu.make_async_copy(wgrad_ref, wgrad_out, sem.at[1]),
    ]
    for copy in copies:
        copy.start()
    for copy in copies:
        copy.wait()


def on_device(
    n_ctx, hidden, queries, key_rows, value_rows, out_grad, doc_ids, q_weight, k_weight, v_weight
):
    tok, head = key_rows.shape
    width = queries.shape[1]
    model = hidden.shape[1]
    heads = width // head
    chips = n_ctx // 2
    vmem = pl.BlockSpec(memory_space=pltpu.VMEM)
    hbm = pl.BlockSpec(memory_space=pl.ANY)
    dma = pltpu.SemaphoreType.DMA
    sums = []
    for lead in ((4, 4, 4), (4, 4), (4,)):
        for first in (lead, (3,) + lead[1:]):
            for block in ((48, head), (48, head), (16, 2 * head)):
                sums.append(pltpu.VMEM(first + block, BF16))
    grads = pl.pallas_call(
        functools.partial(backward_kernel, tok * n_ctx),
        out_shape=(pltpu.VMEM((tok, model), BF16), pltpu.VMEM((64, 2 * head), F32)),
        in_specs=[hbm] * 9,
        out_specs=(vmem, vmem),
        scratch_shapes=[
            pltpu.VMEM((tok, width), BF16),
            pltpu.VMEM((tok, head), BF16),
            pltpu.VMEM((tok, head), BF16),
            pltpu.VMEM((tok, width), BF16),
            pltpu.VMEM((1, tok), jnp.int32),
            pltpu.VMEM((n_ctx, tok + 16, 2 * head), BF16),
            pltpu.VMEM((head, heads * tok), BF16),
            pltpu.VMEM((head, heads * tok), BF16),
            pltpu.VMEM((n_ctx, tok, heads * tok), F32),
            pltpu.VMEM((n_ctx, 1, heads * tok), F32),
            pltpu.VMEM((1, heads * tok), F32),
            pltpu.VMEM((1, heads * tok), F32),
            pltpu.VMEM((tok, heads * tok), BF16),
            pltpu.VMEM((1, heads * tok), F32),
            pltpu.VMEM((head, heads * tok), F32),
            pltpu.VMEM((2, tok, 2 * head), F32),
            pltpu.VMEM((chips, tok, 2 * head), BF16),
            pltpu.VMEM((chips, tok, 2 * head), BF16),
            pltpu.VMEM((chips, tok, 2 * head), BF16),
            pltpu.VMEM((chips, tok, 2 * head), BF16),
            pltpu.VMEM((tok, 2 * head), BF16),
            pltpu.VMEM((model // 128, 2, 64, tok), BF16),
            pltpu.VMEM((model // 128, 64, tok), BF16),
            pltpu.VMEM((model, width), BF16),
            pltpu.VMEM((model, head), BF16),
            pltpu.VMEM((model, head), BF16),
            pltpu.VMEM((tok, width), BF16),
            pltpu.VMEM((2, tok, 2 * head), BF16),
        ] + sums + [
            dma((chips,)), dma((chips,)), dma((1,)), dma((n_ctx,)),
            dma((chips,)), dma((chips,)), dma((chips,)), dma((chips,)), dma((2,)),
            dma((9,)), dma((17,)), dma((17,)), dma((3, 3, 3)), dma((3, 3, 3)),
        ],
        compiler_params=pltpu.CompilerParams(
            collective_id=0, has_side_effects=True, vmem_limit_bytes=56 * 1024 * 1024
        ),
    )(queries, key_rows, value_rows, out_grad, doc_ids.reshape(1, -1),
      hidden, q_weight, k_weight, v_weight)
    return pl.pallas_call(
        finish_kernel,
        out_shape=(
            jax.ShapeDtypeStruct((tok, model), BF16),
            jax.ShapeDtypeStruct((64, 2 * head), F32),
        ),
        in_specs=[vmem] * 2,
        out_specs=(hbm, hbm),
        scratch_shapes=[dma((2,))],
        compiler_params=pltpu.CompilerParams(vmem_limit_bytes=4 * 1024 * 1024),
    )(*grads)


def solution(mesh):
    tokens = P(("dp", "ctx"), None)
    return jax.shard_map(
        functools.partial(on_device, mesh.shape["ctx"]),
        mesh=mesh,
        in_specs=(tokens, tokens, tokens, tokens, tokens, P(("dp", "ctx")), P(), P(), P()),
        out_specs=(tokens, tokens),
        check_vma=False,
    )
```

```python
import functools

import jax
import jax.numpy as jnp
from jax import lax
from jax.experimental import pallas as pl
from jax.experimental.pallas import tpu as pltpu
from jax.sharding import PartitionSpec as P

MESH = pl.DeviceIdType.MESH
BF16 = jnp.bfloat16
F32 = jnp.float32
LOG2E = 1.4426950408889634
MASKED = -1e30


def dot(a, b):
    return jnp.dot(a, b, preferred_element_type=F32)


def dot_rows(a, b):
    return lax.dot_general(a, b, (((1,), (1,)), ((), ())), preferred_element_type=F32)


def backward_kernel(
    seq, q_hbm, k_hbm, v_hbm, do_hbm, docs_hbm, hidden_ref, qw_ref, kw_ref, vw_ref,
    wide, wgrad_ref,
    q_ref, k_ref, v_ref, do_ref, docs_ref, kv, q_t, do_t, probs, max_at, run_max, run_sum, score_grads, delta, dq_t, parts,
    pair_out, pair_in, far_out, far_in, joined,
    hidden_t, hidden_in, qw, kw, vw, dq, dkv,
    sum1_x, sum1_y, sum1_z, got1_x, got1_y, got1_z,
    sum2_x, sum2_y, sum2_z, got2_x, got2_y, got2_z,
    sum3_x, sum3_y, sum3_z, got3_x, got3_y, got3_z,
    kv_send, kv_relay, kv_pass, kv_recv, pair_send, pair_recv, far_send, far_recv, join_send, join_recv,
    load_sem, core_send, core_recv, ring_send, ring_recv,
):
    tok, head = k_ref.shape
    heads = q_ref.shape[1] // head
    chips = kv.shape[0] // 2
    scale = head ** -0.5
    row = lax.axis_index("dp")
    me = lax.axis_index("ctx")
    chip, core = me // 2, me % 2
    other = 1 - core
    partner = chip * 2 + other
    place = (row % 4, (chip % 2) * 2 + row // 4, chip // 2)

    def at(ctx):
        return (row, ctx)

    def along(axis, step):
        x, y, z = [lax.rem(p + step, 4) if i == axis else p for i, p in enumerate(place)]
        return ((y % 2) * 4 + x, z * 4 + (y // 2) * 2 + core)

    barrier = pltpu.get_barrier_semaphore()
    for step in range(1, chips):
        peer = lax.rem(chip + step, chips) * 2 + core
        pl.semaphore_signal(barrier, inc=1, device_id=at(peer), device_id_type=MESH)
    pl.semaphore_signal(barrier, inc=1, device_id=at(partner), device_id_type=MESH)
    for axis, step in ((0, 1), (0, 2), (0, 3), (1, 1), (1, 3)):
        pl.semaphore_signal(barrier, inc=1, device_id=along(axis, step), device_id_type=MESH)

    loads = [
        pltpu.make_async_copy(src, dst, load_sem.at[i])
        for i, (src, dst) in enumerate((
            (k_hbm, k_ref), (v_hbm, v_ref), (docs_hbm, docs_ref), (q_hbm, q_ref), (do_hbm, do_ref),
            (hidden_ref, wide), (qw_ref, qw), (kw_ref, kw), (vw_ref, vw)))
    ]
    for load in loads:
        load.start()
    for load in loads[:3]:
        load.wait()

    kv[me, 0:tok, 0:head] = k_ref[...]
    kv[me, 0:tok, head : 2 * head] = v_ref[...]
    last = docs_ref[...] - row * seq
    high, low = last // 64, last % 64
    digit = lax.broadcasted_iota(jnp.int32, (16, tok), 0)
    kv[me, tok : tok + 16, :] = jnp.where(digit == 0, high, low).astype(F32).astype(BF16)
    own_docs = last.astype(F32)

    def kv_copy(slot, send_sem, target):
        return pltpu.make_async_remote_copy(
            src_ref=kv.at[slot], dst_ref=kv.at[slot], send_sem=send_sem,
            recv_sem=kv_recv.at[slot], device_id=at(target), device_id_type=MESH)

    def pair_copy(index):
        return pltpu.make_async_remote_copy(
            src_ref=pair_out.at[index], dst_ref=pair_in.at[index], send_sem=pair_send.at[index],
            recv_sem=pair_recv.at[index], device_id=at(partner), device_id_type=MESH)

    def far_copy(index, slot):
        return pltpu.make_async_remote_copy(
            src_ref=far_out.at[index], dst_ref=far_in.at[slot], send_sem=far_send.at[index],
            recv_sem=far_recv.at[slot], device_id=at(index * 2 + core), device_id_type=MESH)

    for load in loads[3:5]:
        load.wait()
    for h in range(heads):
        cols = slice(h * head, (h + 1) * head)
        rows = slice(h * tok, (h + 1) * tok)
        q_t[:, rows] = q_ref[:, cols].T
        do_t[:, rows] = do_ref[:, cols].T
    pl.semaphore_wait(barrier, chips + 5)

    plane, side = chip // 2, chip % 2
    neighbour = (2 * plane + 1 - side) * 2 + core
    passes_on = plane >= 2
    passed_chip = (3 - plane) * 2 + side

    def sent_straight(target):
        return (target // 2 + plane != 3) | (target % 2 == side)

    def source_of(back):
        k = back - side
        far_plane = jnp.where((k == 1) | (k == 4), 0, jnp.where(k <= 3, 2, 1))
        far_side = jnp.where((k == 1) | (k == 2) | (k == 5), side, 1 - side)
        near_plane = jnp.where(k <= 2, 1, 0)
        near_side = jnp.where(k % 2 == 1, side, 1 - side)
        return jnp.where(
            (k >= 1) & (plane == 3), 2 * far_plane + far_side,
            jnp.where((k >= 1) & (plane == 2), 2 * near_plane + near_side, chip - back))

    @pl.when(core == 0)
    def _():
        kv_copy(me, kv_send.at[chip], partner).start()

    @pl.loop(0, chips - 1 - chip)
    def _(i):
        target = chips - 1 - i

        @pl.when(sent_straight(target) & (target // 2 != plane + 2))
        def _():
            kv_copy(me, kv_send.at[target], target * 2 + core).start()

    run_max[...] = jnp.full_like(run_max, MASKED)
    run_sum[...] = jnp.zeros_like(run_sum)
    delta[...] = jnp.zeros_like(delta)
    dq_t[...] = jnp.zeros_like(dq_t)

    pieces = 16
    piece_groups = hidden_t.shape[0] // pieces

    def hidden_copy(piece):
        groups = pl.ds(piece * piece_groups, piece_groups)
        return pltpu.make_async_remote_copy(
            src_ref=hidden_t.at[groups, other], dst_ref=hidden_in.at[groups],
            send_sem=core_send.at[piece], recv_sem=core_recv.at[piece],
            device_id=at(partner), device_id_type=MESH)

    @pl.loop(0, 2 * (chip + 1))
    def _(i):
        last_step = i == 2 * chip + 1
        second = jnp.where(last_step | ((i > 0) & (i % 2 == 0)), 1, 0)
        back = jnp.where(last_step, chip, jnp.where(second == 1, i // 2 - 1, (i + 1) // 2))
        source = source_of(back)
        slot = 2 * source + jnp.where(second == 0, core, other)
        skipped = (back == 0) & (second == 1) & (core == 0)

        @pl.when((i > 0) & jnp.logical_not(skipped))
        def _():
            kv_copy(slot, kv_relay.at[source], partner).wait_recv()

        @pl.when((i > 0) & (second == 0))
        def _():
            kv_copy(slot, kv_relay.at[source], partner).start()

        @pl.when((second == 0) & passes_on & (source == passed_chip))
        def _():
            kv_copy(slot, kv_pass.at[0], neighbour).start()

        @pl.when(jnp.logical_not(skipped))
        def _():
            keys = kv[slot, 0:tok, 0:head]
            values = kv[slot, 0:tok, head : 2 * head]
            digits = kv[slot, tok : tok + 16, :].astype(F32)
            key_docs = digits[0:1, :] * 64.0 + digits[1:2, :]
            key_docs = jnp.broadcast_to(key_docs, (tok, tok)).T
            key_pos = lax.broadcasted_iota(jnp.int32, (tok, tok), 0)
            query_pos = lax.broadcasted_iota(jnp.int32, (tok, tok), 1)
            allowed = (key_docs == own_docs) & (key_pos - query_pos <= (me - slot) * tok)
            for h in range(heads):
                rows = slice(h * tok, (h + 1) * tok)
                scores = dot(keys, q_t[:, rows]) * (scale * LOG2E)
                scores = jnp.where(allowed, scores, MASKED)
                old_max = run_max[:, rows]
                new_max = jnp.maximum(old_max, jnp.max(scores, axis=0, keepdims=True))
                weights = jnp.exp2(scores - new_max)
                shrink = jnp.exp2(old_max - new_max)
                run_max[:, rows] = new_max
                max_at[slot, :, rows] = new_max
                run_sum[:, rows] = run_sum[:, rows] * shrink + jnp.sum(weights, axis=0, keepdims=True)
                probs[slot, :, rows] = weights
                prob_grad = dot(values, do_t[:, rows])
                delta[:, rows] = delta[:, rows] * shrink + jnp.sum(
                    weights * prob_grad, axis=0, keepdims=True)

        @pl.when(i == 0)
        def _():
            loads[5].wait()

            @pl.loop(0, hidden_t.shape[0])
            def _(group):
                turned = wide[:, pl.ds(pl.multiple_of(group * 128, 128), 128)].T
                hidden_t[group, 0] = turned[0:64]
                hidden_t[group, 1] = turned[64:128]

            @pl.when(plane < 2)
            def _():
                kv_copy(me, kv_send.at[passed_chip], passed_chip * 2 + core).wait_send()
                for target_side in range(2):
                    target = 2 * (plane + 2) + target_side
                    kv_copy(me, kv_send.at[target], target * 2 + core).start()

    run_sum[...] = 1.0 / run_sum[...]
    delta[...] = delta[...] * run_sum[...]

    def target_of(turn):
        across = (chip + 1) // 2
        own_side = chip % 2
        later = turn - across
        own_plane = jnp.where(plane == 3, jnp.where(later == 0, 2, later - 1), plane - 1 - later)
        return jnp.where(turn == chip, chip, jnp.where(
            turn < across, 2 * turn + 1 - own_side, 2 * own_plane + own_side))

    def joins(target):
        return target // 2 < plane - 1

    def join_copy(index):
        return pltpu.make_async_remote_copy(
            src_ref=far_out.at[2 * index + 1 - side], dst_ref=joined.at[index],
            send_sem=join_send.at[index], recv_sem=join_recv.at[index],
            device_id=at(neighbour), device_id_type=MESH)

    @pl.loop(0, 2 * (chip + 1))
    def _(i):
        turn, second = i // 2, i % 2
        source = target_of(turn)
        slot = 2 * source + jnp.where(second == 0, other, core)
        own_chip = source == chip
        skipped = own_chip & (second == 0) & (core == 0)

        @pl.when(jnp.logical_not(skipped))
        def _():
            keys_t = kv[slot, 0:tok, 0:head].T
            values = kv[slot, 0:tok, head : 2 * head]
            key_part = jnp.zeros((tok, head), F32)
            value_part = jnp.zeros((tok, head), F32)
            for h in range(heads):
                cols = slice(h * head, (h + 1) * head)
                rows = slice(h * tok, (h + 1) * tok)
                factor = jnp.exp2(max_at[slot, :, rows] - run_max[:, rows]) * run_sum[:, rows]
                prob = probs[slot, :, rows] * factor
                prob_grad = dot(values, do_t[:, rows])
                score_grad = (scale * prob * (prob_grad - delta[:, rows])).astype(BF16)
                value_part += dot(prob.astype(BF16), do_ref[:, cols])
                key_part += dot(score_grad, q_ref[:, cols])
                score_grads[:, rows] = score_grad
            dq_t[...] += dot(keys_t, score_grads[...])
            parts[second, :, 0:head] = key_part
            parts[second, :, head : 2 * head] = value_part

        @pl.when((second == 0) & jnp.logical_not(skipped))
        def _():
            pair_out[source] = parts[0].astype(BF16)
            pair_copy(source).start()

        @pl.when((second == 0) & (turn > 0))
        def _():
            before = target_of(turn - 1)
            pair_copy(before).wait_recv()

            @pl.when(joins(before) & (before % 2 == side))
            def _():
                join_copy(before // 2).wait_recv()
                parts[1] += joined[before // 2].astype(F32)

            far_out[before] = (parts[1] + pair_in[before].astype(F32)).astype(BF16)

            @pl.when(joins(before) & (before % 2 != side))
            def _():
                join_copy(before // 2).start()

            @pl.when(jnp.logical_not(joins(before)) | (before % 2 == side))
            def _():
                far_copy(before, chip).start()

        hidden_copy(i).start()

    @pl.loop(2 * (chip + 1), pieces)
    def _(piece):
        hidden_copy(piece).start()

    for h in range(heads):
        cols = slice(h * head, (h + 1) * head)
        rows = slice(h * tok, (h + 1) * tok)
        dq[:, cols] = dq_t[:, rows].T.astype(BF16)

    @pl.when(core == 0)
    def _():
        pair_copy(chip).wait_recv()
        parts[1] += pair_in[chip].astype(F32)

    @pl.loop(chip + 1, chips)
    def _(source):
        @pl.when((plane >= source // 2 - 1) | (source % 2 == side))
        def _():
            far_copy(source, source).wait_recv()
            parts[1] += far_in[source].astype(F32)

    dkv[0] = parts[1].astype(BF16)
    dkv_copy = pltpu.make_async_remote_copy(
        src_ref=dkv.at[0], dst_ref=dkv.at[1], send_sem=core_send.at[pieces],
        recv_sem=core_recv.at[pieces], device_id=at(partner), device_id_type=MESH)
    dkv_copy.start()

    orders = ((0, 1, 2), (1, 2, 0), (2, 0, 1))
    sums = ((sum1_x, sum1_y, sum1_z), (sum2_x, sum2_y, sum2_z), (sum3_x, sum3_y, sum3_z))
    gots = ((got1_x, got1_y, got1_z), (got2_x, got2_y, got2_z), (got3_x, got3_y, got3_z))

    def ring_copy(stage, part, step):
        axis = orders[part][stage]
        return pltpu.make_async_remote_copy(
            src_ref=sums[stage][part].at[lax.rem(place[axis] + step, 4)],
            dst_ref=gots[stage][part].at[step - 1],
            send_sem=ring_send.at[stage, part, step - 1],
            recv_sem=ring_recv.at[stage, part, step - 1],
            device_id=along(axis, step), device_id_type=MESH)

    def quarter_copy(part, step, x):
        axis = orders[part][0]
        return pltpu.make_async_remote_copy(
            src_ref=sums[0][part].at[lax.rem(place[axis] + step, 4), x],
            dst_ref=gots[0][part].at[step - 1, x],
            send_sem=ring_send.at[0, part, step - 1],
            recv_sem=ring_recv.at[0, part, step - 1],
            device_id=along(axis, step), device_id_type=MESH)

    @pl.loop(0, pieces)
    def _(piece):
        hidden_copy(piece).wait_recv()

    for step in range(4):
        x = lax.rem(place[0] + step, 4)
        for y_lo in range(2):
            own = hidden_t[pl.ds(y_lo * 32 + x * 8, 8), core].reshape(512, tok)
            own_terms = dot(own, dkv[0])
            probs[2 * step + y_lo, :, 0 : 2 * head] = own_terms[0:256]
            probs[2 * step + y_lo, :, 2 * head : 4 * head] = own_terms[256:512]
    dkv_copy.wait_recv()
    for step in (2, 1, 3, 0):
        x = lax.rem(place[0] + step, 4)
        for y_lo in range(2):
            paired = hidden_in[pl.ds(y_lo * 32 + x * 8, 8)].reshape(512, tok)
            own_terms = jnp.concatenate(
                [probs[2 * step + y_lo, :, 0 : 2 * head],
                 probs[2 * step + y_lo, :, 2 * head : 4 * head]], axis=0)
            terms = (own_terms + dot(paired, dkv[1])).astype(BF16).reshape(4, 2, 64, 2 * head)
            for y_hi in range(2):
                y = y_hi * 2 + y_lo
                sum1_x[x, y] = terms[:, y_hi, 0:48, 0:head]
                sum1_y[y, x] = terms[:, y_hi, 0:48, head : 2 * head]
                sum1_z[:, x, y] = terms[:, y_hi, 48:64, :]
        if step > 0:
            ring_copy(0, 0, step).start()
        for part in (1, 2):
            for away in (2, 1, 3):
                quarter_copy(part, away, x).start()

    for load in loads[6:]:
        load.wait()
    tile = 512

    @pl.loop(0, wide.shape[1] // tile)
    def _(index):
        rows = pl.ds(pl.multiple_of(index * tile, tile), tile)
        total = dot_rows(dq[...], qw[rows, :])
        total += dot_rows(dkv[0, :, 0:head], kw[rows, :])
        total += dot_rows(dkv[0, :, head : 2 * head], vw[rows, :])
        wide[:, rows] = total.astype(BF16)

    for stage in range(3):
        for part in range(3):
            for step in (1, 3, 2):
                ring_copy(stage, part, step).wait_recv()
            mine = place[orders[part][stage]]
            if stage == 2:
                total = sums[2][part][mine].astype(F32)
                for came in range(3):
                    total += gots[2][part][came].astype(F32)
                wgrad_ref[(slice(0, 48), slice(0, 48), slice(48, 64))[part],
                          (slice(0, head), slice(head, 2 * head), slice(0, 2 * head))[part]] = total
                continue
            for step in (2, 1, 3, 0):
                index = lax.rem(place[orders[part][stage + 1]] + step, 4)
                where = (slice(None), index) if (stage, part) == (0, 1) else (index,)
                total = sums[stage][part][(mine,) + where].astype(F32)
                for came in range(3):
                    total += gots[stage][part][(came,) + where].astype(F32)
                sums[stage + 1][part][index] = total.astype(BF16)
                if step > 0:
                    ring_copy(stage + 1, part, step).start()

    @pl.loop(0, pieces)
    def _(piece):
        hidden_copy(piece).wait_send()

    dkv_copy.wait_send()
    for stage in range(3):
        for part in range(3):
            for step in (1, 2, 3):
                ring_copy(stage, part, step).wait_send()

    @pl.when(core == 0)
    def _():
        kv_copy(me, kv_send.at[chip], partner).wait_send()

    @pl.when(core == 1)
    def _():
        pair_copy(chip).wait_send()

    @pl.loop(chip + 1, chips)
    def _(target):
        @pl.when(sent_straight(target) & ((plane >= 2) | (target != passed_chip)))
        def _():
            kv_copy(me, kv_send.at[target], target * 2 + core).wait_send()

    @pl.when(passes_on)
    def _():
        kv_copy(2 * passed_chip + core, kv_pass.at[0], neighbour).wait_send()

    @pl.loop(0, chip)
    def _(source):
        kv_copy(2 * source + core, kv_relay.at[source], partner).wait_send()
        pair_copy(source).wait_send()

        @pl.when(jnp.logical_not(joins(source)) | (source % 2 == side))
        def _():
            far_copy(source, chip).wait_send()

    @pl.loop(0, jnp.maximum(plane - 1, 0))
    def _(index):
        join_copy(index).wait_send()


def finish_kernel(grad_ref, wgrad_ref, grad_out, wgrad_out, sem):
    copies = [
        pltpu.make_async_copy(grad_ref, grad_out, sem.at[0]),
        pltpu.make_async_copy(wgrad_ref, wgrad_out, sem.at[1]),
    ]
    for copy in copies:
        copy.start()
    for copy in copies:
        copy.wait()


def on_device(
    n_ctx, hidden, queries, key_rows, value_rows, out_grad, doc_ids, q_weight, k_weight, v_weight
):
    tok, head = key_rows.shape
    width = queries.shape[1]
    model = hidden.shape[1]
    heads = width // head
    chips = n_ctx // 2
    vmem = pl.BlockSpec(memory_space=pltpu.VMEM)
    hbm = pl.BlockSpec(memory_space=pl.ANY)
    dma = pltpu.SemaphoreType.DMA
    sums = []
    for lead in ((4, 4, 4), (4, 4), (4,)):
        for first in (lead, (3,) + lead[1:]):
            for block in ((48, head), (48, head), (16, 2 * head)):
                sums.append(pltpu.VMEM(first + block, BF16))
    grads = pl.pallas_call(
        functools.partial(backward_kernel, tok * n_ctx),
        out_shape=(pltpu.VMEM((tok, model), BF16), pltpu.VMEM((64, 2 * head), F32)),
        in_specs=[hbm] * 9,
        out_specs=(vmem, vmem),
        scratch_shapes=[
            pltpu.VMEM((tok, width), BF16),
            pltpu.VMEM((tok, head), BF16),
            pltpu.VMEM((tok, head), BF16),
            pltpu.VMEM((tok, width), BF16),
            pltpu.VMEM((1, tok), jnp.int32),
            pltpu.VMEM((n_ctx, tok + 16, 2 * head), BF16),
            pltpu.VMEM((head, heads * tok), BF16),
            pltpu.VMEM((head, heads * tok), BF16),
            pltpu.VMEM((n_ctx, tok, heads * tok), F32),
            pltpu.VMEM((n_ctx, 1, heads * tok), F32),
            pltpu.VMEM((1, heads * tok), F32),
            pltpu.VMEM((1, heads * tok), F32),
            pltpu.VMEM((tok, heads * tok), BF16),
            pltpu.VMEM((1, heads * tok), F32),
            pltpu.VMEM((head, heads * tok), F32),
            pltpu.VMEM((2, tok, 2 * head), F32),
            pltpu.VMEM((chips, tok, 2 * head), BF16),
            pltpu.VMEM((chips, tok, 2 * head), BF16),
            pltpu.VMEM((chips, tok, 2 * head), BF16),
            pltpu.VMEM((chips, tok, 2 * head), BF16),
            pltpu.VMEM((2, tok, 2 * head), BF16),
            pltpu.VMEM((model // 128, 2, 64, tok), BF16),
            pltpu.VMEM((model // 128, 64, tok), BF16),
            pltpu.VMEM((model, width), BF16),
            pltpu.VMEM((model, head), BF16),
            pltpu.VMEM((model, head), BF16),
            pltpu.VMEM((tok, width), BF16),
            pltpu.VMEM((2, tok, 2 * head), BF16),
        ] + sums + [
            dma((chips,)), dma((chips,)), dma((1,)), dma((n_ctx,)),
            dma((chips,)), dma((chips,)), dma((chips,)), dma((chips,)), dma((2,)), dma((2,)),
            dma((9,)), dma((17,)), dma((17,)), dma((3, 3, 3)), dma((3, 3, 3)),
        ],
        compiler_params=pltpu.CompilerParams(
            collective_id=0, has_side_effects=True, vmem_limit_bytes=56 * 1024 * 1024
        ),
    )(queries, key_rows, value_rows, out_grad, doc_ids.reshape(1, -1),
      hidden, q_weight, k_weight, v_weight)
    return pl.pallas_call(
        finish_kernel,
        out_shape=(
            jax.ShapeDtypeStruct((tok, model), BF16),
            jax.ShapeDtypeStruct((64, 2 * head), F32),
        ),
        in_specs=[vmem] * 2,
        out_specs=(hbm, hbm),
        scratch_shapes=[dma((2,))],
        compiler_params=pltpu.CompilerParams(vmem_limit_bytes=4 * 1024 * 1024),
    )(*grads)


def solution(mesh):
    tokens = P(("dp", "ctx"), None)
    return jax.shard_map(
        functools.partial(on_device, mesh.shape["ctx"]),
        mesh=mesh,
        in_specs=(tokens, tokens, tokens, tokens, tokens, P(("dp", "ctx")), P(), P(), P()),
        out_specs=(tokens, tokens),
        check_vma=False,
    )
```
